32 devices in a mesh: seq: 16 (over z, y, x), batch: 2 (over core).
Axes of the slice: x: 2, y: 2, z: 4, core: 2. Of those that a mesh axis runs over, the one named last changes fastest.
Arguments:
- layer_input_tokens: bfloat16 [16, 4096, 768], P('batch', 'seq'), may hold values from -6 to 6
- cotangent: bfloat16 [16, 4096, 768], P('batch', 'seq'), may hold values from -6 to 6
- weight_in: float32 [768, 3072], P(None, ('seq', 'batch')), may hold values from -0.21875 to 0.21875
- weight_out: float32 [3072, 768], P(('seq', 'batch')), may hold values from -0.109375 to 0.109375
- bias_ff: float32 [3072], P(('seq', 'batch')), may hold values from -1.5 to 1.5
- norm_vec: float32 [5, 768], P(None, ('seq', 'batch')), may hold values from -1.75 to 1.75, as said below
- moment_in: float32 [768, 3072], P(None, ('seq', 'batch')), may hold values from -2 to 2
- average_in: float32 [768, 3072], P(None, ('seq', 'batch')), may hold values from -0.21875 to 0.21875
- moment_out: float32 [3072, 768], P(('seq', 'batch')), may hold values from -4 to 4
- average_out: float32 [3072, 768], P(('seq', 'batch')), may hold values from -0.109375 to 0.109375
- moment_bias: float32 [3072], P(('seq', 'batch')), may hold values from -2 to 2
- average_bias: float32 [3072], P(('seq', 'batch')), may hold values from -1.5 to 1.5
- moment_norm: float32 [5, 768], P(None, ('seq', 'batch')), may hold values from -6 to 6
- average_norm: float32 [5, 768], P(None, ('seq', 'batch')), may hold values from 0.1 to 1.9
Outputs:
- layer_out: float32 [16, 4096, 768], P('batch', 'seq')
- tokens_grad: float32 [16, 4096, 768], P('batch', 'seq')
- moment_in_new: float32 [768, 3072], P(None, ('seq', 'batch'))
- weight_in_new: float32 [768, 3072], P(None, ('seq', 'batch'))
- average_in_new: float32 [768, 3072], P(None, ('seq', 'batch'))
- moment_out_new: float32 [3072, 768], P(('seq', 'batch'))
- weight_out_new: float32 [3072, 768], P(('seq', 'batch'))
- average_out_new: float32 [3072, 768], P(('seq', 'batch'))
- moment_bias_new: float32 [3072], P(('seq', 'batch'))
- bias_ff_new: float32 [3072], P(('seq', 'batch'))
- average_bias_new: float32 [3072], P(('seq', 'batch'))
- moment_norm_new: float32 [5, 768], P(None, ('seq', 'batch'))
- norm_vec_new: float32 [5, 768], P(None, ('seq', 'batch'))
- average_norm_new: float32 [5, 768], P(None, ('seq', 'batch'))
The draws below stay inside these ranges and needn't reach their ends.
Inputs may be any that keep to these rules, and one draw needn't show every extreme that they name: `norm_vec`: rows 0 and 2 are gains between 0.25 and 1.75; rows 1, 3 and 4 are biases.
All inputs are finite; a program needn't handle non-finite values.
Results may differ from the reference program's by a relative error of at most 0.0055.
Values may be sent and summed in bfloat16 or wider, within the bound.
A program may use at most 320 MiB of HBM per device.

```python
import math
import jax
import jax.numpy as jnp
from jax import lax

D = 768
FF = 3072
LEN = 4096
SEQS_ALL = 16
TOKENS = 65536


def draw_norm_vec(key, part):
    key = jax.random.fold_in(key, 11)
    gain_key, bias_random_key = jax.random.split(key)
    gains = jax.random.uniform(gain_key, (2, D), jnp.float32, 0.5, 1.5)
    bias_vectors = jnp.clip(0.3 * jax.random.normal(bias_random_key, (3, D), jnp.float32), -1.2, 1.2)
    return jnp.stack([gains[0], bias_vectors[0], gains[1], bias_vectors[1], bias_vectors[2]], axis=0)


def block_scale(own_key, extent, pieces, smallest, high):
    factor_of, own = 1.0, jax.random.fold_in(own_key, 6)
    for position, blocks in pieces:
        heights = jnp.exp(jax.random.uniform(jax.random.fold_in(own, position), (blocks,), jnp.float32, smallest / len(pieces), high / len(pieces)))
        factor_of = factor_of * jnp.repeat(heights, extent[position] // blocks).reshape([-1 if axis == position else 1 for axis in range(len(extent))])
    return factor_of


def scatter_about(key, shape, deviation, reach, pieces=(), held_as=jnp.bfloat16):
    values = deviation * jax.random.normal(key, shape, jnp.float32)
    if pieces:
        values = values * block_scale(key, shape, pieces, -0.22, 0.18)
    return jnp.clip(values, -reach, reach).astype(held_as)


def setup_inputs(seed: int = 0) -> dict:
    key_of = jax.random.split(jax.random.key(seed), 15)
    return {
        "layer_input_tokens": scatter_about(key_of[0], (SEQS_ALL, LEN, D), 1.0, 6.0, ((0, 2), (1, 16))),
        "cotangent": scatter_about(key_of[1], (SEQS_ALL, LEN, D), 1.0, 6.0, ((0, 2), (1, 16))),
        "weight_in": scatter_about(key_of[2], (D, FF), D ** -0.5, 0.21875, ((1, 32),), jnp.float32),
        "weight_out": scatter_about(key_of[3], (FF, D), FF ** -0.5, 0.109375, ((0, 32),), jnp.float32),
        "bias_ff": scatter_about(key_of[4], (FF,), 0.3, 1.5, ((0, 32),), jnp.float32),
        "norm_vec": draw_norm_vec(jax.random.fold_in(key_of[14], 71), 0),
        "moment_in": scatter_about(key_of[6], (D, FF), 0.35, 2.0, ((1, 32),), jnp.float32),
        "average_in": scatter_about(key_of[7], (D, FF), D ** -0.5, 0.21875, ((1, 32),), jnp.float32),
        "moment_out": scatter_about(key_of[8], (FF, D), 0.65, 4.0, ((0, 32),), jnp.float32),
        "average_out": scatter_about(key_of[9], (FF, D), FF ** -0.5, 0.109375, ((0, 32),), jnp.float32),
        "moment_bias": scatter_about(key_of[10], (FF,), 0.35, 2.0, ((0, 32),), jnp.float32),
        "average_bias": scatter_about(key_of[11], (FF,), 0.3, 1.5, ((0, 32),), jnp.float32),
        "moment_norm": scatter_about(key_of[12], (5, D), 1.0, 6.0, ((1, 32),), jnp.float32),
        "average_norm": jnp.clip(1.0 + 0.18 * jax.random.normal(key_of[13], (5, D), jnp.float32), 0.1, 1.9),
    }


@jax.custom_vjp
def low(v):
    return lax.optimization_barrier(v.astype(jnp.bfloat16)).astype(jnp.float32)

@jax.custom_vjp
def low_back(v):
    return v

def low_keep(v):
    return (low(v), None)

def low_pass(kept, grad):
    return (grad,)

def back_keep(v):
    return (v, None)

def back_low(kept, grad):
    return (low(grad),)
low.defvjp(low_keep, low_pass)
low_back.defvjp(back_keep, back_low)
EPSILON = 1e-05
MOMENTUM = 0.9
AVG_DECAY = 0.9
RATE_MATRIX = 0.02
RATE_VECTOR = 0.1

def trig_pair(width):
    index = jnp.arange(width, dtype=jnp.int32)
    angle = (index[:, None] * index[None, :] % width).astype(jnp.float32) * (2.0 * math.pi / width)
    scale = 1.0 / math.sqrt(width)
    cosine = (jnp.cos(angle) * scale).astype(jnp.bfloat16).astype(jnp.float32)
    sine = (jnp.sin(angle) * scale).astype(jnp.bfloat16).astype(jnp.float32)
    return (cosine, sine)

def matmul(left, right):
    return jnp.dot(left, right, precision=lax.Precision.HIGHEST, preferred_element_type=jnp.float32)

def layer_norm(value, gain, bias):
    center = value - lax.optimization_barrier(jnp.mean(value, axis=-1, keepdims=True))
    spread = lax.optimization_barrier(jnp.mean(center * center, axis=-1, keepdims=True))
    return center * lax.rsqrt(spread + EPSILON) * gain + bias

def reference(layer_input_tokens, cotangent, weight_in, weight_out, bias_ff, norm_vec, moment_in, average_in, moment_out, average_out, moment_bias, average_bias, moment_norm, average_norm):
    cos_hidden, sin_hidden = trig_pair(D)
    cos_seq, sin_seq = trig_pair(LEN)
    hidden_trig_lookup = jnp.concatenate([cos_hidden, sin_hidden], axis=1)
    seq_tab = jnp.concatenate([cos_seq, -sin_seq], axis=1)
    params = (weight_in, weight_out, bias_ff, norm_vec)

    def forward(par, seq_rows):
        w_first, w_second, bias_hidden, vectors = par
        both = low_back(low(matmul(seq_rows, hidden_trig_lookup)))
        stacked = jnp.concatenate([both[:, :D], both[:, D:]], axis=0)
        mixed = low_back(low(matmul(seq_tab, stacked)))
        hidden = layer_norm(seq_rows + mixed, vectors[0], vectors[1])
        hidden_low = low(hidden)
        pre = low_back(matmul(hidden_low, low(w_first)) + bias_hidden)
        act = low(jax.nn.gelu(pre, approximate=False))
        ffo = low_back(matmul(act, low(w_second)) + vectors[4])
        return layer_norm(hidden + ffo, vectors[2], vectors[3])

    def per_sequence(total, inputs):
        seq_rows, seq_cot = inputs
        result, pull = jax.vjp(forward, params, seq_rows)
        dparams, drows = pull(seq_cot)
        total = jax.tree.map(jnp.add, total, dparams)
        return (total, (result, drows))
    zeros = jax.tree.map(jnp.zeros_like, params)
    grads, (layer_out, tokens_grad) = lax.scan(per_sequence, zeros, (layer_input_tokens.astype(jnp.float32), cotangent.astype(jnp.float32)))
    scale = TOKENS ** (-0.5)

    def nesterov(weight, moment, average, grad, rate):
        scaled = grad * scale
        moment_new = MOMENTUM * moment + scaled
        weight_new = weight - rate * (scaled + MOMENTUM * moment_new)
        average_new = AVG_DECAY * average + (1.0 - AVG_DECAY) * weight_new
        return (moment_new, weight_new, average_new)
    m_in, w_in_new, a_in = nesterov(weight_in, moment_in, average_in, grads[0], RATE_MATRIX)
    m_out, w_out_new, a_out = nesterov(weight_out, moment_out, average_out, grads[1], RATE_MATRIX)
    m_bias, b_new, a_bias = nesterov(bias_ff, moment_bias, average_bias, grads[2], RATE_VECTOR)
    m_norm, n_new, a_norm = nesterov(norm_vec, moment_norm, average_norm, grads[3], RATE_VECTOR)
    return (layer_out, tokens_grad, m_in, w_in_new, a_in, m_out, w_out_new, a_out, m_bias, b_new, a_bias, m_norm, n_new, a_norm)
```

```python
import functools
import math

import jax
import jax.numpy as jnp
import ml_dtypes
import numpy as np
from jax import lax
from jax.experimental import pallas as pl
from jax.experimental.pallas import tpu as pltpu
from jax.sharding import PartitionSpec as P

EPSILON = 1e-05
MOMENTUM = 0.9
AVG_DECAY = 0.9
RATE_MATRIX = 0.02
RATE_VECTOR = 0.1
LANES = 128
BLOCK = 256
MESH = pl.DeviceIdType.MESH
F32 = jnp.float32
BF16 = jnp.bfloat16


class Sizes:
    def __init__(self, parts, batch_parts, seqs, local, width, hidden):
        self.parts = parts
        self.batch_parts = batch_parts
        self.seqs = seqs
        self.local = local
        self.width = width
        self.hidden = hidden
        self.length = local * parts
        self.per = width // parts
        self.per_pad = -(-self.per // 16) * 16
        self.rows = self.per_pad + 16
        self.group = max(1, 512 // local)
        self.groups = seqs // self.group
        self.glen = self.group * local
        self.half = local // 2
        self.pack = max(1, LANES // self.half)
        self.depth = parts * LANES
        self.blocks = self.glen // BLOCK
        self.with_batch = batch_parts == 2
        self.seq_bits = parts.bit_length() - 1
        self.bits = self.seq_bits + (1 if self.with_batch else 0)
        self.shards = 1 << self.bits
        self.shard_rows = hidden // self.shards
        self.chunks = hidden // width
        self.chunk_shards = self.shards // self.chunks
        assert parts == 1 << self.seq_bits and self.half * self.pack == LANES
        assert self.group % self.pack == 0 and self.shard_rows % 16 == 0


def mixing_tables(z):
    width, per = z.width, z.per
    index = np.arange(width)
    angle = ((index[:, None] * index[None, :]) % width).astype(np.float32) * np.float32(
        2.0 * math.pi / width
    )
    cosine = np.cos(angle) / np.float32(math.sqrt(width))
    sine = np.sin(angle) / np.float32(math.sqrt(width))
    table = np.zeros((width + 16, width), np.float32)
    joined = np.zeros((width + 16, width), np.float32)
    for owner in range(z.parts):
        for slot in range(per):
            row, j = owner * per + slot, (owner // 2) * per + slot
            if owner % 2 == 0:
                table[row] = cosine[j]
                joined[row, j] = 1.0
                joined[row, (width - j) % width] = 1.0
            elif j > 0:
                table[row] = sine[j]
                joined[row, j] = -1.0
                joined[row, width - j] = 1.0
    table[width] = cosine[width // 2]
    joined[width, width // 2] = 1.0
    order = np.zeros((z.glen, z.glen), np.float32)
    row = 0
    for parity in range(2):
        for seq in range(z.group):
            for i in range(z.half):
                order[row, seq * z.local + 2 * i + parity] = 1.0
                row += 1
    low = ml_dtypes.bfloat16
    return table.astype(low), joined.astype(low), order.astype(low)


def sequence_tables(z):
    wave = (np.arange(z.length).astype(np.float32)) * np.float32(2.0 * math.pi / z.length)
    scale = np.float32(math.sqrt(z.length))
    waves = [
        (np.cos(wave) / scale).astype(ml_dtypes.bfloat16),
        (np.sin(wave) / scale).astype(ml_dtypes.bfloat16),
    ]
    source = np.arange(z.parts)[:, None, None] * z.local + 2 * np.arange(z.half)[None, None, :]
    source = np.broadcast_to(source, (z.parts, z.pack, z.half)).reshape(-1)
    out = np.arange(z.length // 2).reshape(z.parts // 2, z.local)
    result = np.empty((2, z.parts // 2, 2, z.depth, z.local), ml_dtypes.bfloat16)
    for parity in range(2):
        place = ((source + parity)[None, :, None] * out[:, None, :]) % z.length
        for kind in range(2):
            result[kind, :, parity] = waves[kind][place]
    return result


def dot(a, b):
    return jnp.dot(a, b, preferred_element_type=F32)


def dot_nt(a, b):
    return lax.dot_general(a, b, (((1,), (1,)), ((), ())), preferred_element_type=F32)


def dot_tn(a, b):
    return lax.dot_general(a, b, (((0,), (0,)), ((), ())), preferred_element_type=F32)


def normalize(value):
    center = value - jnp.mean(value, axis=-1, keepdims=True)
    spread = jnp.mean(center * center, axis=-1, keepdims=True)
    inverse = lax.rsqrt(spread + EPSILON)
    return center * inverse, inverse


def norm_backward(scaled, normed, inverse):
    return inverse * (
        scaled
        - jnp.mean(scaled, axis=-1, keepdims=True)
        - normed * jnp.mean(scaled * normed, axis=-1, keepdims=True)
    )


def gelu_and_slope(x):
    size = jnp.abs(x)
    t = 1.0 / (1.0 + (0.3275911 * math.sqrt(0.5)) * size)
    bell = jnp.exp(-0.5 * (x * x))
    poly = t * (
        0.5 * 0.254829592
        + t
        * (
            0.5 * -0.284496736
            + t * (0.5 * 1.421413741 + t * (0.5 * -1.453152027 + t * (0.5 * 1.061405429)))
        )
    )
    tail = poly * bell
    phi = jnp.where(x >= 0, 1.0 - tail, tail)
    return x * phi, phi + x * (bell * (1.0 / math.sqrt(2.0 * math.pi)))


KINDS = ("hidden", "gather", "seqmix", "feed", "scatter", "finish")


def plan(z):
    g = z.groups
    gathers = [("gather", i) for i in range(1, z.bits + 1)]
    scatters = [("scatter", i) for i in range(z.bits + 1)]
    steps = [("hidden", 0), gathers.pop(0), ("hidden", 1), gathers.pop(0), ("seqmix", 0)]
    for i in range(2, g):
        if gathers:
            steps.append(gathers.pop(0))
        steps += [("hidden", i), ("seqmix", i - 1)]
    steps += gathers
    back = 0
    for i in range(g):
        steps.append(("feed", i))
        if i == 0:
            steps.append(("seqmix", g - 1))
        if i >= 2:
            steps.append(("seqmix", g + back))
            back += 1
    steps.append(scatters.pop(0))
    done = 0
    while back < g:
        steps.append(("seqmix", g + back))
        back += 1
        if scatters:
            steps.append(scatters.pop(0))
        if done < back - 1:
            steps.append(("finish", done))
            done += 1
    while done < g:
        if scatters:
            steps.append(scatters.pop(0))
        steps.append(("finish", done))
        done += 1
    return steps + scatters


def step_kernel(
    z,
    x_hbm,
    cot_hbm,
    shard_in,
    shard_out,
    shard_vec,
    seq_table,
    table,
    joined,
    order,
    result_hbm,
    grad_hbm,
    total_in,
    total_out,
    total_vec,
    landed,
    full_in,
    full_out,
    full_vec,
    sum_in,
    sum_out,
    bias,
    vectors,
    vec_sum,
    vec_land,
    recv_a,
    recv_b,
    send,
    recv_sa,
    recv_sb,
    send_sa,
    send_sb,
    lhs,
    slots,
    source,
    xs,
    cs,
    act,
    slope,
    normed_one,
    hidden,
    low,
    dlow,
    work,
    stage,
    inverse_one,
    sem_a,
    sem_b,
    sem_send,
    sem_sa,
    sem_sb,
    sem_ssa,
    sem_ssb,
    sem_gather_send,
    sem_gather_recv,
    sem_scatter_send,
    sem_scatter_recv,
    sem_local,
    sem_slot,
):
    parts, per, groups = z.parts, z.per, z.groups
    me = lax.axis_index("seq")
    core = lax.axis_index("batch")
    fulls = (full_in, full_out, full_vec)
    sums = (sum_in, sum_out)
    vec_lanes = z.hidden + z.width

    own = [lax.rem(lax.div(me, 1 << (z.seq_bits - 1 - d)), 2) for d in range(z.seq_bits)]
    own += [core] if z.with_batch else []
    weights = [1 << (z.bits - 1 - d) for d in range(z.bits)]
    first = list(range(z.bits))
    second = list(first)
    a, b = z.seq_bits - 2, z.seq_bits - 1
    second[a], second[b] = second[b], second[a]
    gather_orders = (first, second, first)

    def partner(d):
        if d < z.seq_bits:
            return (me + (1 - 2 * own[d]) * (1 << (z.seq_bits - 1 - d)), core)
        return (me, 1 - core)

    def shard_at(free, k, flipped=None):
        index = 0
        for d in range(z.bits):
            if d in free:
                value = lax.rem(lax.div(k, 1 << free.index(d)), 2)
            elif d == flipped:
                value = 1 - own[d]
            else:
                value = own[d]
            index = index + value * weights[d]
        return index

    barrier = pltpu.get_barrier_semaphore()

    def greet(d, carry):
        pl.semaphore_signal(
            barrier, inc=1, device_id=(lax.rem(me + d, parts), core), device_id_type=MESH
        )
        return carry

    lax.fori_loop(1, parts, greet, 0)
    if z.with_batch:
        pl.semaphore_signal(barrier, inc=1, device_id=(me, 1 - core), device_id_type=MESH)
    greeted = parts - 1 + (1 if z.with_batch else 0)

    mine = shard_at((), 0)
    for w, shard in enumerate((shard_in, shard_out, shard_vec)):
        pltpu.make_async_copy(shard, fulls[w].at[mine], sem_local.at[w]).start()
    lhs[...] = jnp.zeros_like(lhs)
    send_sa[...] = jnp.zeros_like(send_sa)
    vec_sum[...] = jnp.zeros_like(vec_sum)

    @pl.when(me != 0)
    def _():
        recv_sa[...] = jnp.zeros_like(recv_sa)

    pl.semaphore_wait(barrier, greeted)

    def gather_send(stage_no):
        for w in range(3):
            order_w = gather_orders[w]
            free, d = order_w[:stage_no], order_w[stage_no]

            def body(k, carry, w=w, free=free, d=d):
                at = shard_at(free, k)
                pltpu.make_async_remote_copy(
                    src_ref=fulls[w].at[at],
                    dst_ref=fulls[w].at[at],
                    send_sem=sem_gather_send.at[w, stage_no],
                    recv_sem=sem_gather_recv.at[w, stage_no],
                    device_id=partner(d),
                    device_id_type=MESH,
                ).start()
                return carry

            lax.fori_loop(0, 1 << stage_no, body, 0)

    def gather_wait(stage_no):
        for w in range(3):
            some = fulls[w].at[pl.ds(0, 1 << stage_no)]
            pltpu.make_async_copy(some, some, sem_gather_recv.at[w, stage_no]).wait()

    def gather_done():
        for stage_no in range(z.bits):
            for w in range(3):
                some = fulls[w].at[pl.ds(0, 1 << stage_no)]
                pltpu.make_async_copy(some, some, sem_gather_send.at[w, stage_no]).wait()

    for w, shard in enumerate((shard_in, shard_out, shard_vec)):
        pltpu.make_async_copy(shard, fulls[w].at[mine], sem_local.at[w]).wait()
    gather_send(0)

    def gather_step(i):
        for stage_no in range(1, z.bits + 1):

            @pl.when(i == stage_no)
            def _(stage_no=stage_no):
                gather_wait(stage_no - 1)
                if stage_no < z.bits:
                    gather_send(stage_no)
                else:
                    gather_done()
                    place_vectors()

    def place_vectors():
        none = jnp.zeros((8, z.width - LANES), F32)
        lane = lax.broadcasted_iota(jnp.int32, (8, z.width), 1)
        wide = z.shard_rows
        narrow = z.width // z.shards
        for c in range(z.chunks):
            line = jnp.zeros((8, z.width), F32)
            for i in range(z.chunk_shards):
                row = jnp.concatenate([full_vec[c * z.chunk_shards + i, 0:8], none], axis=1)
                row = jnp.where(lane < wide, row, 0.0)
                line = line + (pltpu.roll(row, i * wide, 1) if i else row)
            bias[:, c * z.width : (c + 1) * z.width] = line[0:1]
        line = jnp.zeros((8, z.width), F32)
        for i in range(z.shards):
            row = jnp.concatenate([full_vec[i, 8:16], none], axis=1)
            row = jnp.where(lane < narrow, row, 0.0)
            line = line + (pltpu.roll(row, i * narrow, 1) if i else row)
        vectors[...] = line

    def wait_all(ref, sem):
        pltpu.make_async_copy(ref, ref, sem).wait()

    def wait_sent(g):
        some = send.at[g, pl.ds(0, parts - 1)]
        pltpu.make_async_copy(some, some, sem_send.at[g]).wait()

    def push(g, peer, landing, sem):
        @pl.when(peer != me)
        def _():
            pltpu.make_async_remote_copy(
                src_ref=send.at[g, peer],
                dst_ref=landing.at[g, me],
                send_sem=sem_send.at[g],
                recv_sem=sem.at[g],
                device_id=(peer, core),
                device_id_type=MESH,
            ).start()

        @pl.when(peer == me)
        def _():
            pltpu.make_async_copy(send.at[g, me], landing.at[g, me], sem.at[g]).start()

    def hidden_step(u):
        g = lax.rem(u, groups)
        tokens = pl.ds(pl.multiple_of(g * z.glen, z.glen), z.glen)

        @pl.when(u < groups)
        def _():
            copy = pltpu.make_async_copy(x_hbm.at[tokens], source, sem_local.at[3])
            copy.start()
            copy.wait()

        moved = dot(order[...], source[...]).astype(BF16)
        out = dot_nt(table[...], moved)

        @pl.when(u >= groups)
        def _():
            wait_sent(g)

            @pl.when(me != 0)
            def _():
                wait_all(send_sa.at[g], sem_ssa.at[g])

        send[g] = out[: z.width].reshape(parts, per, z.glen).astype(BF16)
        last = out[z.width : z.width + 1].astype(BF16).astype(F32)
        for r in range(z.glen // LANES):
            send_sa[g, r : r + 1, :] = last[:, r * LANES : (r + 1) * LANES]

        @pl.when(me != 0)
        def _():
            pltpu.make_async_remote_copy(
                src_ref=send_sa.at[g],
                dst_ref=recv_sa.at[g, me],
                send_sem=sem_ssa.at[g],
                recv_sem=sem_sa.at[g],
                device_id=(0, core),
                device_id_type=MESH,
            ).start()

        @pl.when(me == 0)
        def _():
            pltpu.make_async_copy(send_sa.at[g], recv_sa.at[g, 0], sem_sa.at[g]).start()

        def body(d, carry):
            push(g, lax.rem(me + d, parts), recv_a, sem_a)
            return carry

        lax.fori_loop(0, parts, body, 0)

    def seqmix_step(u):
        g = lax.rem(u, groups)
        kind = lax.rem(me, 2)
        half_parts = parts // 2

        def fetch(j):
            which = lax.rem(me + j, half_parts)
            return pltpu.make_async_copy(
                seq_table.at[kind, which], slots.at[lax.rem(j, 2)], sem_slot.at[lax.rem(j, 2)]
            )

        fetch(0).start()
        wait_all(recv_a.at[g], sem_a.at[g])

        @pl.when(me == 0)
        def _():
            wait_all(recv_sa.at[g], sem_sa.at[g])

        def gather_rows(c, carry):
            columns = pl.ds(pl.multiple_of(c * LANES, LANES), LANES)
            for parity in range(2):
                for s in range(z.group):
                    at = parity * (z.group // z.pack) + s // z.pack
                    rows = recv_a[g, c, :, at * LANES : (at + 1) * LANES]
                    line = jnp.broadcast_to(recv_sa[g, c, at : at + 1, :], (16, LANES)).astype(BF16)
                    if z.pack > 1:
                        lane = lax.broadcasted_iota(jnp.int32, (per, LANES), 1) // z.half
                        rows = jnp.where(lane == s % z.pack, rows.astype(F32), 0.0).astype(BF16)
                        lane = lax.broadcasted_iota(jnp.int32, (16, LANES), 1) // z.half
                        line = jnp.where(lane == s % z.pack, line.astype(F32), 0.0).astype(BF16)
                    lhs[parity, s, 0:per, columns] = rows
                    lhs[parity, s, z.per_pad : z.rows, columns] = line
            return carry

        lax.fori_loop(0, parts, gather_rows, 0)
        wait_sent(g)

        @pl.when((me == 0) & (u >= groups))
        def _():
            some = send_sb.at[g, pl.ds(0, parts - 1)]
            pltpu.make_async_copy(some, some, sem_ssb.at[g]).wait()

        def body(j, carry):
            @pl.when(j + 1 < half_parts)
            def _():
                fetch(j + 1).start()

            fetch(j).wait()
            slot = lax.rem(j, 2)
            near = lax.rem(me + j, half_parts)
            even = dot(lhs[0].reshape(z.group * z.rows, z.depth), slots[slot, 0])
            odd = dot(lhs[1].reshape(z.group * z.rows, z.depth), slots[slot, 1])
            for peer, value in ((near, even + odd), (near + half_parts, even - odd)):
                value = value.reshape(z.group, z.rows, z.local)
                for s in range(z.group):
                    lanes = slice(s * z.local, (s + 1) * z.local)
                    send[g, peer, :, lanes] = value[s, :per].astype(BF16)
                    for r in range(z.local // LANES):
                        at = s * (z.local // LANES) + r
                        send_sb[g, peer, at : at + 1, :] = value[
                            s, z.per_pad : z.per_pad + 1, r * LANES : (r + 1) * LANES
                        ]
                push(g, peer, recv_b, sem_b)

                @pl.when((me == 0) & (peer != 0))
                def _(peer=peer):
                    pltpu.make_async_remote_copy(
                        src_ref=send_sb.at[g, peer],
                        dst_ref=recv_sb.at[g],
                        send_sem=sem_ssb.at[g],
                        recv_sem=sem_sb.at[g],
                        device_id=(peer, core),
                        device_id_type=MESH,
                    ).start()

                @pl.when((me == 0) & (peer == 0))
                def _():
                    pltpu.make_async_copy(send_sb.at[g, 0], recv_sb.at[g], sem_sb.at[g]).start()

            return carry

        lax.fori_loop(0, half_parts, body, 0)

    def mixed_block(g, t):
        lanes = pl.ds(pl.multiple_of(t * BLOCK, BLOCK), BLOCK)
        rows = recv_b[g, :, :, lanes]
        if per % 16:
            rows = rows.astype(F32).reshape(z.width, BLOCK).astype(BF16)
        else:
            rows = rows.reshape(z.width, BLOCK)
        line = jnp.concatenate(
            [recv_sb[g, pl.ds(t * (BLOCK // LANES) + r, 1), :] for r in range(BLOCK // LANES)], axis=1
        )
        line = jnp.broadcast_to(line, (16, BLOCK)).astype(BF16)
        return dot_tn(rows, joined[: z.width]) + dot_tn(line, joined[z.width :])

    def mixed_wait(g):
        wait_all(recv_b.at[g], sem_b.at[g])
        wait_all(recv_sb.at[g], sem_sb.at[g])

    def feed_step(g):
        tokens = pl.ds(pl.multiple_of(g * z.glen, z.glen), z.glen)
        load_x = pltpu.make_async_copy(x_hbm.at[tokens], xs, sem_local.at[4])
        load_c = pltpu.make_async_copy(cot_hbm.at[tokens], cs, sem_local.at[5])
        load_x.start()
        load_c.start()
        mixed_wait(g)
        load_x.wait()
        load_c.wait()

        def block(t, carry):
            rows = pl.ds(pl.multiple_of(t * BLOCK, BLOCK), BLOCK)
            outer = pl.ds(pl.multiple_of(g * z.glen + t * BLOCK, BLOCK), BLOCK)
            value = xs[rows, :].astype(F32) + mixed_block(g, t)
            normed, inverse = normalize(value)
            normed_one[...] = normed
            inverse_one[...] = inverse
            value = normed * vectors[0:1, :] + vectors[1:2, :]
            hidden[...] = value
            low[...] = value.astype(BF16)
            work[...] = jnp.zeros_like(work)

            def forward(c, carry):
                lanes = pl.ds(pl.multiple_of(c * z.width, z.width), z.width)
                some = pl.ds(c * z.chunk_shards, z.chunk_shards)
                pre = dot_nt(low[...], full_in[some].reshape(z.width, z.width)) + bias[:, lanes]
                value, pull = gelu_and_slope(pre)
                value = value.astype(BF16)
                act[:, lanes] = value
                slope[:, lanes] = pull.astype(BF16)
                work[...] += dot(value, full_out[some].reshape(z.width, z.width))
                return carry

            lax.fori_loop(0, z.chunks, forward, 0)
            normed, inverse = normalize(hidden[...] + (work[...] + vectors[4:5, :]))
            stage[...] = normed * vectors[2:3, :] + vectors[3:4, :]
            put = pltpu.make_async_copy(stage, result_hbm.at[outer], sem_local.at[6])
            put.start()
            grad = cs[rows, :].astype(F32)
            here = pl.ds(z.hidden, z.width)
            vec_sum[2:3, here] += jnp.sum(grad * normed, axis=0, keepdims=True)
            vec_sum[3:4, here] += jnp.sum(grad, axis=0, keepdims=True)
            grad = norm_backward(grad * vectors[2:3, :], normed, inverse)
            work[...] = grad
            dffo = grad.astype(BF16)
            dlow[...] = dffo
            vec_sum[4:5, here] += jnp.sum(dffo.astype(F32), axis=0, keepdims=True)

            def backward(c, carry):
                lanes = pl.ds(pl.multiple_of(c * z.width, z.width), z.width)
                some = pl.ds(c * z.chunk_shards, z.chunk_shards)
                shape = (z.chunk_shards, z.shard_rows, z.width)
                dpre = dot_nt(dlow[...], full_out[some].reshape(z.width, z.width))
                dpre = (dpre * slope[:, lanes].astype(F32)).astype(BF16)
                vec_sum[0:1, lanes] += jnp.sum(dpre.astype(F32), axis=0, keepdims=True)
                work[...] += dot(dpre, full_in[some].reshape(z.width, z.width))
                into_out = dot_tn(act[:, lanes], dlow[...]).reshape(shape)
                into_in = dot_tn(dpre, low[...]).reshape(shape)

                @pl.when(g + t == 0)
                def _():
                    sum_out[some] = into_out
                    sum_in[some] = into_in

                @pl.when(g + t > 0)
                def _():
                    sum_out[some] += into_out
                    sum_in[some] += into_in

                return carry

            lax.fori_loop(0, z.chunks, backward, 0)
            grad, normed = work[...], normed_one[...]
            vec_sum[0:1, here] += jnp.sum(grad * normed, axis=0, keepdims=True)
            vec_sum[1:2, here] += jnp.sum(grad, axis=0, keepdims=True)
            grad = norm_backward(grad * vectors[0:1, :], normed, inverse_one[...])
            source[rows, :] = grad.astype(BF16)
            put.wait()
            stage[...] = grad
            put = pltpu.make_async_copy(stage, grad_hbm.at[outer], sem_local.at[6])
            put.start()
            put.wait()
            return carry

        lax.fori_loop(0, z.blocks, block, 0)
        hidden_step(g + groups)

    def finish_step(g):
        def load(t):
            outer = pl.ds(pl.multiple_of(g * z.glen + t * BLOCK, BLOCK), BLOCK)
            return pltpu.make_async_copy(grad_hbm.at[outer], work, sem_local.at[7])

        load(0).start()
        mixed_wait(g)

        def block(t, carry):
            outer = pl.ds(pl.multiple_of(g * z.glen + t * BLOCK, BLOCK), BLOCK)

            @pl.when(t > 0)
            def _():
                load(t).start()

            value = mixed_block(g, t)
            load(t).wait()
            stage[...] = work[...] + value
            put = pltpu.make_async_copy(stage, grad_hbm.at[outer], sem_local.at[6])
            put.start()
            put.wait()
            return carry

        lax.fori_loop(0, z.blocks, block, 0)

    offsets = [sum(1 << (z.bits - 1 - i) for i in range(s)) for s in range(z.bits)]

    def scatter_orders(w):
        if w < 2:
            return gather_orders[w][::-1]
        return gather_orders[0][::-1]

    def scatter_send(s):
        count = 1 << (z.bits - 1 - s)
        for w in range(2):
            path = scatter_orders(w)
            d, free = path[s], path[s + 1 :]

            def body(k, carry, w=w, d=d, free=free):
                at = shard_at(free, k, flipped=d)
                fulls[w][at] = sums[w][at].astype(BF16)
                pltpu.make_async_remote_copy(
                    src_ref=fulls[w].at[at],
                    dst_ref=landed.at[w, offsets[s] + k],
                    send_sem=sem_scatter_send.at[w, s],
                    recv_sem=sem_scatter_recv.at[w, s],
                    device_id=partner(d),
                    device_id_type=MESH,
                ).start()
                return carry

            lax.fori_loop(0, count, body, 0)
        pltpu.make_async_remote_copy(
            src_ref=vec_sum,
            dst_ref=vec_land.at[s],
            send_sem=sem_scatter_send.at[2, s],
            recv_sem=sem_scatter_recv.at[2, s],
            device_id=partner(scatter_orders(2)[s]),
            device_id_type=MESH,
        ).start()

    def scatter_add(s):
        count = 1 << (z.bits - 1 - s)
        for w in range(2):
            path = scatter_orders(w)
            free = path[s + 1 :]
            some = landed.at[w, pl.ds(offsets[s], count)]
            wait_all(some, sem_scatter_recv.at[w, s])

            def fetch(k, carry, w=w, free=free):
                pltpu.make_async_copy(
                    landed.at[w, offsets[s] + k], fulls[w].at[shard_at(free, k)], sem_local.at[w]
                ).start()
                return carry

            lax.fori_loop(0, count, fetch, 0)
        wait_all(vec_sum, sem_scatter_send.at[2, s])
        wait_all(vec_land.at[s], sem_scatter_recv.at[2, s])
        vec_sum[...] += vec_land[s]
        for w in range(2):
            free = scatter_orders(w)[s + 1 :]
            some = landed.at[w, pl.ds(offsets[s], count)]
            wait_all(some, sem_local.at[w])

            def add(k, carry, w=w, free=free):
                at = shard_at(free, k)
                sums[w][at] += fulls[w][at].astype(F32)
                return carry

            lax.fori_loop(0, count, add, 0)

    def scatter_step(i):
        for s in range(z.bits + 1):

            @pl.when(i == s)
            def _(s=s):
                if s > 0:
                    scatter_add(s - 1)
                if s < z.bits:
                    scatter_send(s)

    steps = plan(z)
    bodies = (hidden_step, gather_step, seqmix_step, feed_step, scatter_step, finish_step)

    def one_step(s, carry):
        kind, argument = 0, 0
        for i, (name, value) in enumerate(steps):
            here = (s == i).astype(jnp.int32)
            kind = kind + here * KINDS.index(name)
            argument = argument + here * value
        for k, body in enumerate(bodies):

            @pl.when(kind == k)
            def _(body=body):
                body(argument)

        return carry

    lax.fori_loop(0, len(steps), one_step, 0)

    for w, total in ((0, total_in), (1, total_out)):
        pltpu.make_async_copy(sums[w].at[mine], total, sem_local.at[w]).start()
    pltpu.make_async_copy(vec_sum, total_vec, sem_local.at[2]).start()
    for g in range(groups):
        wait_sent(g)

        @pl.when(me != 0)
        def _(g=g):
            wait_all(send_sa.at[g], sem_ssa.at[g])

        @pl.when(me == 0)
        def _(g=g):
            some = send_sb.at[g, pl.ds(0, parts - 1)]
            pltpu.make_async_copy(some, some, sem_ssb.at[g]).wait()

    for s in range(z.bits):
        for w in range(2):
            some = landed.at[w, pl.ds(offsets[s], 1 << (z.bits - 1 - s))]
            wait_all(some, sem_scatter_send.at[w, s])
    for w, total in ((0, total_in), (1, total_out)):
        pltpu.make_async_copy(sums[w].at[mine], total, sem_local.at[w]).wait()
    pltpu.make_async_copy(vec_sum, total_vec, sem_local.at[2]).wait()


def run_step(z, x, cot, shard_in, shard_out, shard_vec, tables):
    tokens = z.seqs * z.local
    vec_lanes = z.hidden + z.width
    shard = (z.shards, z.shard_rows, z.width)
    block = (BLOCK, z.width)
    any_space, vmem = pl.BlockSpec(memory_space=pl.ANY), pl.BlockSpec(memory_space=pltpu.VMEM)
    dma = pltpu.SemaphoreType.DMA
    g = z.groups
    scratch = [
        pltpu.VMEM(shard, BF16),
        pltpu.VMEM(shard, BF16),
        pltpu.VMEM((z.shards, 16, LANES), F32),
        pltpu.VMEM(shard, F32),
        pltpu.VMEM(shard, F32),
        pltpu.VMEM((1, z.hidden), F32),
        pltpu.VMEM((8, z.width), F32),
        pltpu.VMEM((8, vec_lanes), F32),
        pltpu.VMEM((z.bits, 8, vec_lanes), F32),
        pltpu.VMEM((g, z.parts, z.per, z.glen), BF16),
        pltpu.VMEM((g, z.parts, z.per, z.glen), BF16),
        pltpu.VMEM((g, z.parts, z.per, z.glen), BF16),
        pltpu.VMEM((g, z.parts, 8, LANES), F32),
        pltpu.VMEM((g, 8, LANES), F32),
        pltpu.VMEM((g, 8, LANES), F32),
        pltpu.VMEM((g, z.parts, 8, LANES), F32),
        pltpu.VMEM((2, z.group, z.rows, z.depth), BF16),
        pltpu.VMEM((2, 2, z.depth, z.local), BF16),
        pltpu.VMEM((z.glen, z.width), BF16),
        pltpu.VMEM((z.glen, z.width), BF16),
        pltpu.VMEM((z.glen, z.width), BF16),
        pltpu.VMEM((BLOCK, z.hidden), BF16),
        pltpu.VMEM((BLOCK, z.hidden), BF16),
        pltpu.VMEM(block, F32),
        pltpu.VMEM(block, F32),
        pltpu.VMEM(block, BF16),
        pltpu.VMEM(block, BF16),
        pltpu.VMEM(block, F32),
        pltpu.VMEM(block, F32),
        pltpu.VMEM((BLOCK, 1), F32),
        dma((g,)),
        dma((g,)),
        dma((g,)),
        dma((g,)),
        dma((g,)),
        dma((g,)),
        dma((g,)),
        dma((3, z.bits)),
        dma((3, z.bits)),
        dma((3, z.bits)),
        dma((3, z.bits)),
        dma((8,)),
        dma((2,)),
    ]
    return pl.pallas_call(
        functools.partial(step_kernel, z),
        out_shape=(
            jax.ShapeDtypeStruct((tokens, z.width), F32),
            jax.ShapeDtypeStruct((tokens, z.width), F32),
            jax.ShapeDtypeStruct(shard[1:], F32),
            jax.ShapeDtypeStruct(shard[1:], F32),
            jax.ShapeDtypeStruct((8, vec_lanes), F32),
            jax.ShapeDtypeStruct((2, z.shards - 1) + shard[1:], BF16),
        ),
        in_specs=[any_space] * 6 + [vmem] * 3,
        out_specs=(any_space,) * 6,
        scratch_shapes=scratch,
        compiler_params=pltpu.CompilerParams(
            collective_id=0, has_side_effects=True, vmem_limit_bytes=64 << 20
        ),
        cost_estimate=pl.CostEstimate(
            flops=12 * tokens * z.width * z.hidden + 16 * tokens * z.width * z.length // 16,
            bytes_accessed=40 * tokens * z.width,
            transcendentals=tokens * z.hidden,
        ),
    )(x, cot, shard_in, shard_out, shard_vec, *tables)


def nesterov(weight, moment, average, grad, rate, scale):
    scaled = grad * scale
    moment_new = MOMENTUM * moment + scaled
    weight_new = weight - rate * (scaled + MOMENTUM * moment_new)
    average_new = AVG_DECAY * average + (1.0 - AVG_DECAY) * weight_new
    return (moment_new, weight_new, average_new)


def on_device(
    seq_parts,
    batch_parts,
    layer_input_tokens,
    cotangent,
    weight_in,
    weight_out,
    bias_ff,
    norm_vec,
    moment_in,
    average_in,
    moment_out,
    average_out,
    moment_bias,
    average_bias,
    moment_norm,
    average_norm,
):
    seqs, local, width = layer_input_tokens.shape
    devices = seq_parts * batch_parts
    hidden = weight_out.shape[0] * devices
    z = Sizes(seq_parts, batch_parts, seqs, local, width, hidden)
    tokens = seqs * local

    shard_in = weight_in.T.astype(BF16)
    shard_out = weight_out.astype(BF16)
    bias_shard, norm_shard = bias_ff, norm_vec
    if not z.with_batch:
        shard_in, shard_out, bias_shard = (
            lax.all_gather(v, "batch", axis=0, tiled=True) for v in (shard_in, shard_out, bias_shard)
        )
        norm_shard = lax.all_gather(norm_shard, "batch", axis=1, tiled=True)
    bias_line = jnp.pad(bias_shard[None, :], ((0, 7), (0, LANES - bias_shard.shape[0])))
    norm_rows = jnp.pad(norm_shard, ((0, 3), (0, LANES - norm_shard.shape[1])))
    shard_vec = jnp.concatenate([bias_line, norm_rows], axis=0)

    tables = [jnp.asarray(sequence_tables(z))] + [jnp.asarray(t) for t in mixing_tables(z)]
    result, tokens_grad, grad_in, grad_out, grad_vec, _ = run_step(
        z,
        layer_input_tokens.reshape(tokens, width),
        cotangent.reshape(tokens, width),
        shard_in,
        shard_out,
        shard_vec,
        tables,
    )
    index = lax.axis_index("seq") * batch_parts + lax.axis_index("batch")
    if not z.with_batch:
        grad_in = lax.psum_scatter(grad_in, "batch", scatter_dimension=0, tiled=True)
        grad_out = lax.psum_scatter(grad_out, "batch", scatter_dimension=0, tiled=True)
        grad_vec = lax.psum(grad_vec, "batch")
    count, narrow = hidden // devices, width // devices
    grad_bias = lax.dynamic_slice(grad_vec[0], (index * count,), (count,))
    grad_norm = lax.dynamic_slice(grad_vec[:5], (0, hidden + index * narrow), (5, narrow))

    scale = (seqs * batch_parts * local * seq_parts) ** (-0.5)
    m_in, w_in_new, a_in = nesterov(
        weight_in, moment_in, average_in, grad_in.T, RATE_MATRIX, scale
    )
    m_out, w_out_new, a_out = nesterov(
        weight_out, moment_out, average_out, grad_out, RATE_MATRIX, scale
    )
    m_bias, b_new, a_bias = nesterov(
        bias_ff, moment_bias, average_bias, grad_bias, RATE_VECTOR, scale
    )
    m_norm, n_new, a_norm = nesterov(
        norm_vec, moment_norm, average_norm, grad_norm, RATE_VECTOR, scale
    )
    return (
        result.reshape(seqs, local, width),
        tokens_grad.reshape(seqs, local, width),
        m_in,
        w_in_new,
        a_in,
        m_out,
        w_out_new,
        a_out,
        m_bias,
        b_new,
        a_bias,
        m_norm,
        n_new,
        a_norm,
    )


def solution(mesh):
    tokens = P("batch", "seq", None)
    columns, rows, flat = P(None, ("seq", "batch")), P(("seq", "batch"), None), P(("seq", "batch"))
    return jax.shard_map(
        functools.partial(on_device, mesh.shape["seq"], mesh.shape["batch"]),
        mesh=mesh,
        in_specs=(tokens, tokens, columns, rows, flat, columns)
        + (columns, columns, rows, rows, flat, flat, columns, columns),
        out_specs=(tokens, tokens)
        + (columns,) * 3
        + (rows,) * 3
        + (flat,) * 3
        + (columns,) * 3,
        check_vma=False,
    )
```

```python
import functools
import math

import jax
import jax.numpy as jnp
import ml_dtypes
import numpy as np
from jax import lax
from jax.experimental import pallas as pl
from jax.experimental.pallas import tpu as pltpu
from jax.sharding import PartitionSpec as P

EPSILON = 1e-05
MOMENTUM = 0.9
AVG_DECAY = 0.9
RATE_MATRIX = 0.02
RATE_VECTOR = 0.1
LANES = 128
MESH = pl.DeviceIdType.MESH
F32 = jnp.float32
BF16 = jnp.bfloat16


class Sizes:
    def __init__(self, parts, batch_parts, seqs, local, width, hidden):
        self.parts = parts
        self.batch_parts = batch_parts
        self.seqs = seqs
        self.local = local
        self.width = width
        self.hidden = hidden
        self.length = local * parts
        self.per = width // parts
        self.per_pad = -(-self.per // 16) * 16
        self.rows = self.per_pad + 16
        self.group = max(1, 512 // local)
        self.groups = seqs // self.group
        self.glen = self.group * local
        self.half = local // 2
        self.pack = max(1, LANES // self.half)
        self.depth = parts * LANES
        self.pair = 2 if self.groups % 2 == 0 and self.depth <= 2048 else 1
        self.pairs = self.groups // self.pair
        self.lhs_rows = 2 * self.pair * self.group * self.rows
        self.shared = self.lhs_rows <= self.glen and self.depth <= hidden
        self.with_batch = batch_parts == 2
        self.seq_bits = parts.bit_length() - 1
        self.bits = self.seq_bits + (1 if self.with_batch else 0)
        self.shards = 1 << self.bits
        self.shard_rows = hidden // self.shards
        self.chunks = hidden // width
        self.chunk_shards = self.shards // self.chunks
        assert parts == 1 << self.seq_bits and self.half * self.pack == LANES
        assert self.group % self.pack == 0 and self.shard_rows % 16 == 0


def mixing_tables(z):
    width, per = z.width, z.per
    index = np.arange(width)
    angle = ((index[:, None] * index[None, :]) % width).astype(np.float32) * np.float32(
        2.0 * math.pi / width
    )
    cosine = np.cos(angle) / np.float32(math.sqrt(width))
    sine = np.sin(angle) / np.float32(math.sqrt(width))
    table = np.zeros((width + 16, width), np.float32)
    joined = np.zeros((width + 16, width), np.float32)
    for owner in range(z.parts):
        for slot in range(per):
            row, j = owner * per + slot, (owner // 2) * per + slot
            if owner % 2 == 0:
                table[row] = cosine[j]
                joined[row, j] = 1.0
                joined[row, (width - j) % width] = 1.0
            elif j > 0:
                table[row] = sine[j]
                joined[row, j] = -1.0
                joined[row, width - j] = 1.0
    table[width] = cosine[width // 2]
    joined[width, width // 2] = 1.0
    order = np.zeros((z.glen, z.glen), np.float32)
    row = 0
    for parity in range(2):
        for seq in range(z.group):
            for i in range(z.half):
                order[row, seq * z.local + 2 * i + parity] = 1.0
                row += 1
    low = ml_dtypes.bfloat16
    return table.astype(low), joined.astype(low), order.astype(low)


def sequence_tables(z):
    wave = (np.arange(z.length).astype(np.float32)) * np.float32(2.0 * math.pi / z.length)
    scale = np.float32(math.sqrt(z.length))
    waves = [
        (np.cos(wave) / scale).astype(ml_dtypes.bfloat16),
        (np.sin(wave) / scale).astype(ml_dtypes.bfloat16),
    ]
    source = np.arange(z.parts)[:, None, None] * z.local + 2 * np.arange(z.half)[None, None, :]
    source = np.broadcast_to(source, (z.parts, z.pack, z.half)).reshape(-1)
    out = np.arange(z.length // 2).reshape(z.parts // 2, z.local)
    result = np.empty((2, z.parts // 2, 2, z.depth, z.local), ml_dtypes.bfloat16)
    for parity in range(2):
        place = ((source + parity)[None, :, None] * out[:, None, :]) % z.length
        for kind in range(2):
            result[kind, :, parity] = waves[kind][place]
    return result


def dot(a, b):
    return jnp.dot(a, b, preferred_element_type=F32)


def dot_nt(a, b):
    return lax.dot_general(a, b, (((1,), (1,)), ((), ())), preferred_element_type=F32)


def dot_tn(a, b):
    return lax.dot_general(a, b, (((0,), (0,)), ((), ())), preferred_element_type=F32)


def normalize(value):
    center = value - jnp.mean(value, axis=-1, keepdims=True)
    spread = jnp.mean(center * center, axis=-1, keepdims=True)
    inverse = lax.rsqrt(spread + EPSILON)
    return center * inverse, inverse


def norm_backward(scaled, normed, inverse):
    return inverse * (
        scaled
        - jnp.mean(scaled, axis=-1, keepdims=True)
        - normed * jnp.mean(scaled * normed, axis=-1, keepdims=True)
    )


def gelu_and_slope(x):
    size = jnp.abs(x)
    t = 1.0 / (1.0 + (0.3275911 * math.sqrt(0.5)) * size)
    bell = jnp.exp(-0.5 * (x * x))
    poly = t * (
        0.5 * 0.254829592
        + t
        * (
            0.5 * -0.284496736
            + t * (0.5 * 1.421413741 + t * (0.5 * -1.453152027 + t * (0.5 * 1.061405429)))
        )
    )
    tail = poly * bell
    phi = jnp.where(x >= 0, 1.0 - tail, tail)
    return x * phi, phi + x * (bell * (1.0 / math.sqrt(2.0 * math.pi)))


STEPS = {"H": "hidden", "G": "gather", "T": "pair", "t": "single", "F": "feed", "S": "scatter", "E": "finish"}
KINDS = tuple(STEPS.values())


ORDER = (
    "G1", "H0", "G2", "H1", "G3", "H2", "H3", "T0", "G4", "T1", "G5",
    "F0", "F1", "F2", "T2", "F3", "S0", "t6", "S1", "S2", "t7", "E0",
    "S3", "E1", "E2", "S4", "E3", "S5",
)


def plan(z):
    if (z.groups, z.pairs, z.bits) == (4, 2, 5):
        return [(STEPS[name[0]], int(name[1:])) for name in ORDER]
    g = z.groups
    steps = [("hidden", i) for i in range(g)] + [("gather", i) for i in range(1, z.bits + 1)]
    steps += [("single", i) for i in range(g)] + [("feed", i) for i in range(g)]
    steps += [("scatter", 0)] + [("single", g + i) for i in range(g)]
    steps += [("scatter", i) for i in range(1, z.bits + 1)]
    return steps + [("finish", i) for i in range(g)]


def step_kernel(
    z,
    x_hbm,
    cot_hbm,
    shard_in,
    shard_out,
    shard_vec,
    seq_table,
    table,
    joined,
    order,
    result_hbm,
    grad_hbm,
    total_in,
    total_out,
    total_vec,
    landed,
    full_in,
    full_out,
    full_vec,
    sum_in,
    sum_out,
    bias,
    vectors,
    vec_sum,
    vec_land,
    recv_a,
    recv_b,
    send,
    recv_sa,
    recv_sb,
    send_sa,
    send_sb,
    own_lhs,
    slots,
    source,
    cs,
    act,
    slope,
    normed_one,
    low,
    dlow,
    work,
    stage,
    inverse_one,
    sem_a,
    sem_b,
    sem_send,
    sem_sa,
    sem_sb,
    sem_ssa,
    sem_ssb,
    sem_gather_send,
    sem_gather_recv,
    sem_scatter_send,
    sem_scatter_recv,
    sem_local,
    sem_slot,
):
    parts, per, groups = z.parts, z.per, z.groups
    me = lax.axis_index("seq")
    core = lax.axis_index("batch")
    fulls = (full_in, full_out, full_vec)
    sums = (sum_in, sum_out)
    lhs = act if z.shared else own_lhs

    own = [lax.rem(lax.div(me, 1 << (z.seq_bits - 1 - d)), 2) for d in range(z.seq_bits)]
    own += [core] if z.with_batch else []
    weights = [1 << (z.bits - 1 - d) for d in range(z.bits)]
    first = list(range(z.bits))
    second = list(first)
    a, b = z.seq_bits - 2, z.seq_bits - 1
    second[a], second[b] = second[b], second[a]
    gather_orders = (first, second, first)

    def partner(d):
        if d < z.seq_bits:
            return (me + (1 - 2 * own[d]) * (1 << (z.seq_bits - 1 - d)), core)
        return (me, 1 - core)

    def shard_at(free, k, flipped=None):
        index = 0
        for d in range(z.bits):
            if d in free:
                value = lax.rem(lax.div(k, 1 << free.index(d)), 2)
            elif d == flipped:
                value = 1 - own[d]
            else:
                value = own[d]
            index = index + value * weights[d]
        return index

    barrier = pltpu.get_barrier_semaphore()

    def greet(d, carry):
        pl.semaphore_signal(
            barrier, inc=1, device_id=(lax.rem(me + d, parts), core), device_id_type=MESH
        )
        return carry

    lax.fori_loop(1, parts, greet, 0)
    if z.with_batch:
        pl.semaphore_signal(barrier, inc=1, device_id=(me, 1 - core), device_id_type=MESH)
    greeted = parts - 1 + (1 if z.with_batch else 0)

    mine = shard_at((), 0)
    for w, shard in enumerate((shard_in, shard_out, shard_vec)):
        pltpu.make_async_copy(shard, fulls[w].at[mine], sem_local.at[w]).start()
    send_sa[...] = jnp.zeros_like(send_sa)
    vec_sum[...] = jnp.zeros_like(vec_sum)

    @pl.when(me != 0)
    def _():
        recv_sa[...] = jnp.zeros_like(recv_sa)

    pl.semaphore_wait(barrier, greeted)

    def gather_send(stage_no):
        for w in range(3):
            order_w = gather_orders[w]
            free, d = order_w[:stage_no], order_w[stage_no]

            def body(k, carry, w=w, free=free, d=d):
                at = shard_at(free, k)
                pltpu.make_async_remote_copy(
                    src_ref=fulls[w].at[at],
                    dst_ref=fulls[w].at[at],
                    send_sem=sem_gather_send.at[w, stage_no],
                    recv_sem=sem_gather_recv.at[w, stage_no],
                    device_id=partner(d),
                    device_id_type=MESH,
                ).start()
                return carry

            lax.fori_loop(0, 1 << stage_no, body, 0)

    def gather_wait(stage_no):
        for w in range(3):
            some = fulls[w].at[pl.ds(0, 1 << stage_no)]
            pltpu.make_async_copy(some, some, sem_gather_recv.at[w, stage_no]).wait()

    def gather_done():
        for stage_no in range(z.bits):
            for w in range(3):
                some = fulls[w].at[pl.ds(0, 1 << stage_no)]
                pltpu.make_async_copy(some, some, sem_gather_send.at[w, stage_no]).wait()

    for w, shard in enumerate((shard_in, shard_out, shard_vec)):
        pltpu.make_async_copy(shard, fulls[w].at[mine], sem_local.at[w]).wait()
    gather_send(0)

    def gather_step(i):
        for stage_no in range(1, z.bits + 1):

            @pl.when(i == stage_no)
            def _(stage_no=stage_no):
                gather_wait(stage_no - 1)
                if stage_no < z.bits:
                    gather_send(stage_no)
                else:
                    gather_done()
                    place_vectors()

    def place_vectors():
        none = jnp.zeros((8, z.width - LANES), F32)
        lane = lax.broadcasted_iota(jnp.int32, (8, z.width), 1)
        wide = z.shard_rows
        narrow = z.width // z.shards
        for c in range(z.chunks):
            line = jnp.zeros((8, z.width), F32)
            for i in range(z.chunk_shards):
                row = jnp.concatenate([full_vec[c * z.chunk_shards + i, 0:8], none], axis=1)
                row = jnp.where(lane < wide, row, 0.0)
                line = line + (pltpu.roll(row, i * wide, 1) if i else row)
            bias[:, c * z.width : (c + 1) * z.width] = line[0:1]
        line = jnp.zeros((8, z.width), F32)
        for i in range(z.shards):
            row = jnp.concatenate([full_vec[i, 8:16], none], axis=1)
            row = jnp.where(lane < narrow, row, 0.0)
            line = line + (pltpu.roll(row, i * narrow, 1) if i else row)
        vectors[...] = line

    def wait_all(ref, sem):
        pltpu.make_async_copy(ref, ref, sem).wait()

    def wait_sent(g):
        some = send.at[g, pl.ds(0, parts - 1)]
        pltpu.make_async_copy(some, some, sem_send.at[g]).wait()

    def push(g, peer, landing, sem):
        @pl.when(peer != me)
        def _():
            pltpu.make_async_remote_copy(
                src_ref=send.at[g, peer],
                dst_ref=landing.at[g, me],
                send_sem=sem_send.at[g],
                recv_sem=sem.at[g],
                device_id=(peer, core),
                device_id_type=MESH,
            ).start()

        @pl.when(peer == me)
        def _():
            pltpu.make_async_copy(send.at[g, me], landing.at[g, me], sem.at[g]).start()

    def hidden_step(u):
        g = lax.rem(u, groups)
        tokens = pl.ds(pl.multiple_of(g * z.glen, z.glen), z.glen)

        @pl.when(u < groups)
        def _():
            copy = pltpu.make_async_copy(x_hbm.at[tokens], source, sem_local.at[3])
            copy.start()
            copy.wait()

        moved = dot(order[...], source[...]).astype(BF16)
        out = dot_nt(table[...], moved)

        @pl.when(u >= groups)
        def _():
            wait_sent(g)

            @pl.when(me != 0)
            def _():
                wait_all(send_sa.at[g], sem_ssa.at[g])

        send[g] = out[: z.width].reshape(parts, per, z.glen).astype(BF16)
        last = out[z.width : z.width + 1].astype(BF16).astype(F32)
        for r in range(z.glen // LANES):
            send_sa[g, r : r + 1, :] = last[:, r * LANES : (r + 1) * LANES]

        @pl.when(me != 0)
        def _():
            pltpu.make_async_remote_copy(
                src_ref=send_sa.at[g],
                dst_ref=recv_sa.at[g, me],
                send_sem=sem_ssa.at[g],
                recv_sem=sem_sa.at[g],
                device_id=(0, core),
                device_id_type=MESH,
            ).start()

        @pl.when(me == 0)
        def _():
            pltpu.make_async_copy(send_sa.at[g], recv_sa.at[g, 0], sem_sa.at[g]).start()

        def body(d, carry):
            push(g, lax.rem(me + d, parts), recv_a, sem_a)
            return carry

        lax.fori_loop(0, parts, body, 0)

    half_parts = parts // 2
    deep = z.depth // 2

    def fetch(j, quarter):
        return pltpu.make_async_copy(
            seq_table.at[
                lax.rem(me, 2),
                lax.rem(me + j, half_parts),
                quarter // 2,
                pl.ds(quarter % 2 * deep, deep),
            ],
            slots.at[quarter],
            sem_slot.at[quarter],
        )

    def pair_step(u):
        first = lax.rem(u, z.pairs) * z.pair
        sequence_transform([first + q for q in range(z.pair)], u >= z.pairs)

    def single_step(u):
        sequence_transform([lax.rem(u, groups)], u >= groups)

    def sequence_transform(members, returning):
        seqs = len(members) * z.group

        for q, g in enumerate(members):
            wait_all(recv_a.at[g], sem_a.at[g])

            @pl.when(me == 0)
            def _(g=g):
                wait_all(recv_sa.at[g], sem_sa.at[g])

            def gather_rows(c, carry, q=q, g=g):
                columns = pl.ds(pl.multiple_of(c * LANES, LANES), LANES)
                for parity in range(2):
                    for s in range(z.group):
                        at = parity * (z.group // z.pack) + s // z.pack
                        rows = recv_a[g, c, :, at * LANES : (at + 1) * LANES]
                        line = recv_sa[g, c, at : at + 1, :]
                        line = jnp.broadcast_to(line, (16, LANES)).astype(BF16)
                        if z.pack > 1:
                            lane = lax.broadcasted_iota(jnp.int32, (per, LANES), 1) // z.half
                            rows = jnp.where(lane == s % z.pack, rows.astype(F32), 0.0).astype(BF16)
                            lane = lax.broadcasted_iota(jnp.int32, (16, LANES), 1) // z.half
                            line = jnp.where(lane == s % z.pack, line.astype(F32), 0.0).astype(BF16)
                        base = (parity * seqs + q * z.group + s) * z.rows
                        lhs[base : base + per, columns] = rows
                        lhs[base + z.per_pad : base + z.rows, columns] = line
                return carry

            lax.fori_loop(0, parts, gather_rows, 0)
            wait_sent(g)

            @pl.when((me == 0) & returning)
            def _(g=g):
                some = send_sb.at[g, pl.ds(0, parts - 1)]
                pltpu.make_async_copy(some, some, sem_ssb.at[g]).wait()

        def push_both(g, peer):
            push(g, peer, recv_b, sem_b)

            @pl.when((me == 0) & (peer != 0))
            def _():
                pltpu.make_async_remote_copy(
                    src_ref=send_sb.at[g, peer],
                    dst_ref=recv_sb.at[g],
                    send_sem=sem_ssb.at[g],
                    recv_sem=sem_sb.at[g],
                    device_id=(peer, core),
                    device_id_type=MESH,
                ).start()

            @pl.when((me == 0) & (peer == 0))
            def _():
                pltpu.make_async_copy(send_sb.at[g, 0], recv_sb.at[g], sem_sb.at[g]).start()

        def body(j, carry):
            near = lax.rem(me + j, half_parts)
            halves = []
            for parity in range(2):
                total = 0.0
                for quarter in (2 * parity, 2 * parity + 1):
                    fetch(j, quarter).wait()
                    lanes = slice(quarter % 2 * deep, (quarter % 2 + 1) * deep)
                    rows = lhs[parity * seqs * z.rows : (parity + 1) * seqs * z.rows, lanes]
                    total = total + dot(rows, slots[quarter])

                    fetch(j + 1, quarter).start()

                halves.append(total.reshape(seqs, z.rows, z.local))

            even, odd = halves
            for peer, value in ((near, even + odd), (near + half_parts, even - odd)):
                for q, g in enumerate(members):
                    for s in range(z.group):
                        part = value[q * z.group + s]
                        lanes = slice(s * z.local, (s + 1) * z.local)
                        send[g, peer, :, lanes] = part[:per].astype(BF16)
                        for r in range(z.local // LANES):
                            at = s * (z.local // LANES) + r
                            send_sb[g, peer, at : at + 1, :] = part[
                                z.per_pad : z.per_pad + 1, r * LANES : (r + 1) * LANES
                            ]
                push_both(members[0], peer)
            return carry

        lax.fori_loop(0, half_parts, body, 0)
        for g in members[1:]:

            def later(d, carry, g=g):
                push_both(g, lax.rem(me + d, parts))
                return carry

            lax.fori_loop(0, parts, later, 0)

    def mixed(g):
        wait_all(recv_b.at[g], sem_b.at[g])
        wait_all(recv_sb.at[g], sem_sb.at[g])
        rows = recv_b[g]
        if per % 16:
            rows = rows.astype(F32).reshape(z.width, z.glen).astype(BF16)
        else:
            rows = rows.reshape(z.width, z.glen)
        line = jnp.concatenate([recv_sb[g, r : r + 1, :] for r in range(z.glen // LANES)], axis=1)
        line = jnp.broadcast_to(line, (16, z.glen)).astype(BF16)
        return dot_tn(rows, joined[: z.width]) + dot_tn(line, joined[z.width :])

    def tokens_of(g):
        return pl.ds(pl.multiple_of(g * z.glen, z.glen), z.glen)

    def feed_step(g):
        load_x = pltpu.make_async_copy(x_hbm.at[tokens_of(g)], source, sem_local.at[4])
        load_c = pltpu.make_async_copy(cot_hbm.at[tokens_of(g)], cs, sem_local.at[5])
        put_result = pltpu.make_async_copy(stage, result_hbm.at[tokens_of(g)], sem_local.at[6])
        put_grad = pltpu.make_async_copy(work, grad_hbm.at[tokens_of(g)], sem_local.at[7])
        load_x.start()
        load_c.start()
        value = mixed(g)
        load_x.wait()
        load_c.wait()
        normed, inverse = normalize(source[...].astype(F32) + value)
        normed_one[...] = normed
        inverse_one[...] = inverse
        low[...] = (normed * vectors[0:1, :] + vectors[1:2, :]).astype(BF16)
        work[...] = jnp.zeros_like(work)

        def forward(c, carry):
            lanes = pl.ds(pl.multiple_of(c * z.width, z.width), z.width)
            some = pl.ds(c * z.chunk_shards, z.chunk_shards)
            pre = dot_nt(low[...], full_in[some].reshape(z.width, z.width)) + bias[:, lanes]
            value, pull = gelu_and_slope(pre)
            value = value.astype(BF16)
            act[:, lanes] = value
            slope[:, lanes] = pull.astype(BF16)
            work[...] += dot(value, full_out[some].reshape(z.width, z.width))
            return carry

        lax.fori_loop(0, z.chunks, forward, 0, unroll=2)
        value = normed_one[...] * vectors[0:1, :] + vectors[1:2, :]
        normed, inverse = normalize(value + (work[...] + vectors[4:5, :]))
        stage[...] = normed * vectors[2:3, :] + vectors[3:4, :]
        put_result.start()
        grad = cs[...].astype(F32)
        here = pl.ds(z.hidden, z.width)
        vec_sum[2:3, here] += jnp.sum(grad * normed, axis=0, keepdims=True)
        vec_sum[3:4, here] += jnp.sum(grad, axis=0, keepdims=True)
        grad = norm_backward(grad * vectors[2:3, :], normed, inverse)
        work[...] = grad
        dffo = grad.astype(BF16)
        dlow[...] = dffo
        vec_sum[4:5, here] += jnp.sum(dffo.astype(F32), axis=0, keepdims=True)

        def backward(c, carry):
            lanes = pl.ds(pl.multiple_of(c * z.width, z.width), z.width)
            some = pl.ds(c * z.chunk_shards, z.chunk_shards)
            shape = (z.chunk_shards, z.shard_rows, z.width)
            dpre = dot_nt(dlow[...], full_out[some].reshape(z.width, z.width))
            dpre = (dpre * slope[:, lanes].astype(F32)).astype(BF16)
            vec_sum[0:1, lanes] += jnp.sum(dpre.astype(F32), axis=0, keepdims=True)
            work[...] += dot(dpre, full_in[some].reshape(z.width, z.width))
            into_out = dot_tn(act[:, lanes], dlow[...]).reshape(shape)
            into_in = dot_tn(dpre, low[...]).reshape(shape)

            @pl.when(g == 0)
            def _():
                sum_out[some] = into_out
                sum_in[some] = into_in

            @pl.when(g > 0)
            def _():
                sum_out[some] += into_out
                sum_in[some] += into_in

            return carry

        lax.fori_loop(0, z.chunks, backward, 0)
        grad, normed = work[...], normed_one[...]
        vec_sum[0:1, here] += jnp.sum(grad * normed, axis=0, keepdims=True)
        vec_sum[1:2, here] += jnp.sum(grad, axis=0, keepdims=True)
        grad = norm_backward(grad * vectors[0:1, :], normed, inverse_one[...])
        source[...] = grad.astype(BF16)
        work[...] = grad
        put_grad.start()
        hidden_step(g + groups)
        put_result.wait()
        put_grad.wait()

    def finish_put(g):
        return pltpu.make_async_copy(stage, grad_hbm.at[tokens_of(g)], sem_local.at[6])

    def finish_step(g):
        load = pltpu.make_async_copy(grad_hbm.at[tokens_of(g)], work, sem_local.at[7])
        load.start()
        value = mixed(g)
        load.wait()

        @pl.when(g > 0)
        def _():
            finish_put(g - 1).wait()

        stage[...] = work[...] + value
        finish_put(g).start()

    offsets = [sum(1 << (z.bits - 1 - i) for i in range(s)) for s in range(z.bits)]

    def scatter_orders(w):
        if w < 2:
            return gather_orders[w][::-1]
        return gather_orders[0][::-1]

    def scatter_send(s):
        count = 1 << (z.bits - 1 - s)
        for w in range(2):
            path = scatter_orders(w)
            d, free = path[s], path[s + 1 :]

            def body(k, carry, w=w, d=d, free=free):
                at = shard_at(free, k, flipped=d)
                fulls[w][at] = sums[w][at].astype(BF16)
                pltpu.make_async_remote_copy(
                    src_ref=fulls[w].at[at],
                    dst_ref=landed.at[w, offsets[s] + k],
                    send_sem=sem_scatter_send.at[w, s],
                    recv_sem=sem_scatter_recv.at[w, s],
                    device_id=partner(d),
                    device_id_type=MESH,
                ).start()
                return carry

            lax.fori_loop(0, count, body, 0)
        pltpu.make_async_remote_copy(
            src_ref=vec_sum,
            dst_ref=vec_land.at[s],
            send_sem=sem_scatter_send.at[2, s],
            recv_sem=sem_scatter_recv.at[2, s],
            device_id=partner(scatter_orders(2)[s]),
            device_id_type=MESH,
        ).start()

    def scatter_add(s):
        count = 1 << (z.bits - 1 - s)
        for w in range(2):
            path = scatter_orders(w)
            free = path[s + 1 :]
            some = landed.at[w, pl.ds(offsets[s], count)]
            wait_all(some, sem_scatter_recv.at[w, s])

            def fetch(k, carry, w=w, free=free):
                pltpu.make_async_copy(
                    landed.at[w, offsets[s] + k], fulls[w].at[shard_at(free, k)], sem_local.at[w]
                ).start()
                return carry

            lax.fori_loop(0, count, fetch, 0)
        wait_all(vec_sum, sem_scatter_send.at[2, s])
        wait_all(vec_land.at[s], sem_scatter_recv.at[2, s])
        vec_sum[...] += vec_land[s]
        for w in range(2):
            free = scatter_orders(w)[s + 1 :]
            some = landed.at[w, pl.ds(offsets[s], count)]
            wait_all(some, sem_local.at[w])

            def add(k, carry, w=w, free=free):
                at = shard_at(free, k)
                sums[w][at] += fulls[w][at].astype(F32)
                return carry

            lax.fori_loop(0, count, add, 0)

    def scatter_step(i):
        for s in range(z.bits + 1):

            @pl.when(i == s)
            def _(s=s):
                if s > 0:
                    scatter_add(s - 1)
                if s < z.bits:
                    scatter_send(s)

    steps = plan(z)
    bodies = (
        hidden_step,
        gather_step,
        pair_step,
        single_step,
        feed_step,
        scatter_step,
        finish_step,
    )
    used = {name for name, _ in steps}

    def one_step(s, carry):
        kind, argument = 0, 0
        for i, (name, value) in enumerate(steps):
            here = (s == i).astype(jnp.int32)
            kind = kind + here * KINDS.index(name)
            argument = argument + here * value
        for k, body in enumerate(bodies):
            if KINDS[k] not in used:
                continue

            @pl.when(kind == k)
            def _(body=body):
                body(argument)

        return carry

    for quarter in range(4):
        fetch(0, quarter).start()
    lax.fori_loop(0, len(steps), one_step, 0)
    for quarter in range(4):
        fetch(0, quarter).wait()

    for w, total in ((0, total_in), (1, total_out)):
        pltpu.make_async_copy(sums[w].at[mine], total, sem_local.at[w]).start()
    pltpu.make_async_copy(vec_sum, total_vec, sem_local.at[2]).start()
    finish_put(groups - 1).wait()
    for g in range(groups):
        wait_sent(g)

        @pl.when(me != 0)
        def _(g=g):
            wait_all(send_sa.at[g], sem_ssa.at[g])

        @pl.when(me == 0)
        def _(g=g):
            some = send_sb.at[g, pl.ds(0, parts - 1)]
            pltpu.make_async_copy(some, some, sem_ssb.at[g]).wait()

    for s in range(z.bits):
        for w in range(2):
            some = landed.at[w, pl.ds(offsets[s], 1 << (z.bits - 1 - s))]
            wait_all(some, sem_scatter_send.at[w, s])
    for w, total in ((0, total_in), (1, total_out)):
        pltpu.make_async_copy(sums[w].at[mine], total, sem_local.at[w]).wait()
    pltpu.make_async_copy(vec_sum, total_vec, sem_local.at[2]).wait()


def run_step(z, x, cot, shard_in, shard_out, shard_vec, tables):
    tokens = z.seqs * z.local
    vec_lanes = z.hidden + z.width
    shard = (z.shards, z.shard_rows, z.width)
    block = (z.glen, z.width)
    any_space, vmem = pl.BlockSpec(memory_space=pl.ANY), pl.BlockSpec(memory_space=pltpu.VMEM)
    dma = pltpu.SemaphoreType.DMA
    g = z.groups
    scratch = [
        pltpu.VMEM(shard, BF16),
        pltpu.VMEM(shard, BF16),
        pltpu.VMEM((z.shards, 16, LANES), F32),
        pltpu.VMEM(shard, F32),
        pltpu.VMEM(shard, F32),
        pltpu.VMEM((1, z.hidden), F32),
        pltpu.VMEM((8, z.width), F32),
        pltpu.VMEM((8, vec_lanes), F32),
        pltpu.VMEM((z.bits, 8, vec_lanes), F32),
        pltpu.VMEM((g, z.parts, z.per, z.glen), BF16),
        pltpu.VMEM((g, z.parts, z.per, z.glen), BF16),
        pltpu.VMEM((g, z.parts, z.per, z.glen), BF16),
        pltpu.VMEM((g, z.parts, 8, LANES), F32),
        pltpu.VMEM((g, 8, LANES), F32),
        pltpu.VMEM((g, 8, LANES), F32),
        pltpu.VMEM((g, z.parts, 8, LANES), F32),
        pltpu.VMEM((16, LANES) if z.shared else (z.lhs_rows, z.depth), BF16),
        pltpu.VMEM((4, z.depth // 2, z.local), BF16),
        pltpu.VMEM((z.glen, z.width), BF16),
        pltpu.VMEM((z.glen, z.width), BF16),
        pltpu.VMEM((z.glen, z.hidden), BF16),
        pltpu.VMEM((z.glen, z.hidden), BF16),
        pltpu.VMEM(block, F32),
        pltpu.VMEM(block, BF16),
        pltpu.VMEM(block, BF16),
        pltpu.VMEM(block, F32),
        pltpu.VMEM(block, F32),
        pltpu.VMEM((z.glen, 1), F32),
        dma((g,)),
        dma((g,)),
        dma((g,)),
        dma((g,)),
        dma((g,)),
        dma((g,)),
        dma((g,)),
        dma((3, z.bits)),
        dma((3, z.bits)),
        dma((3, z.bits)),
        dma((3, z.bits)),
        dma((8,)),
        dma((4,)),
    ]
    return pl.pallas_call(
        functools.partial(step_kernel, z),
        out_shape=(
            jax.ShapeDtypeStruct((tokens, z.width), F32),
            jax.ShapeDtypeStruct((tokens, z.width), F32),
            jax.ShapeDtypeStruct(shard[1:], F32),
            jax.ShapeDtypeStruct(shard[1:], F32),
            jax.ShapeDtypeStruct((8, vec_lanes), F32),
            jax.ShapeDtypeStruct((2, z.shards - 1) + shard[1:], BF16),
        ),
        in_specs=[any_space] * 6 + [vmem] * 3,
        out_specs=(any_space,) * 6,
        scratch_shapes=scratch,
        compiler_params=pltpu.CompilerParams(
            collective_id=0, has_side_effects=True, vmem_limit_bytes=64 << 20
        ),
        cost_estimate=pl.CostEstimate(
            flops=12 * tokens * z.width * z.hidden + 16 * tokens * z.width * z.length // 16,
            bytes_accessed=40 * tokens * z.width,
            transcendentals=tokens * z.hidden,
        ),
    )(x, cot, shard_in, shard_out, shard_vec, *tables)


def nesterov(weight, moment, average, grad, rate, scale):
    scaled = grad * scale
    moment_new = MOMENTUM * moment + scaled
    weight_new = weight - rate * (scaled + MOMENTUM * moment_new)
    average_new = AVG_DECAY * average + (1.0 - AVG_DECAY) * weight_new
    return (moment_new, weight_new, average_new)


def on_device(
    seq_parts,
    batch_parts,
    layer_input_tokens,
    cotangent,
    weight_in,
    weight_out,
    bias_ff,
    norm_vec,
    moment_in,
    average_in,
    moment_out,
    average_out,
    moment_bias,
    average_bias,
    moment_norm,
    average_norm,
):
    seqs, local, width = layer_input_tokens.shape
    devices = seq_parts * batch_parts
    hidden = weight_out.shape[0] * devices
    z = Sizes(seq_parts, batch_parts, seqs, local, width, hidden)
    tokens = seqs * local

    shard_in = weight_in.T.astype(BF16)
    shard_out = weight_out.astype(BF16)
    bias_shard, norm_shard = bias_ff, norm_vec
    if not z.with_batch:
        shard_in, shard_out, bias_shard = (
            lax.all_gather(v, "batch", axis=0, tiled=True) for v in (shard_in, shard_out, bias_shard)
        )
        norm_shard = lax.all_gather(norm_shard, "batch", axis=1, tiled=True)
    bias_line = jnp.pad(bias_shard[None, :], ((0, 7), (0, LANES - bias_shard.shape[0])))
    norm_rows = jnp.pad(norm_shard, ((0, 3), (0, LANES - norm_shard.shape[1])))
    shard_vec = jnp.concatenate([bias_line, norm_rows], axis=0)

    tables = [jnp.asarray(sequence_tables(z))] + [jnp.asarray(t) for t in mixing_tables(z)]
    result, tokens_grad, grad_in, grad_out, grad_vec, _ = run_step(
        z,
        layer_input_tokens.reshape(tokens, width),
        cotangent.reshape(tokens, width),
        shard_in,
        shard_out,
        shard_vec,
        tables,
    )
    index = lax.axis_index("seq") * batch_parts + lax.axis_index("batch")
    if not z.with_batch:
        grad_in = lax.psum_scatter(grad_in, "batch", scatter_dimension=0, tiled=True)
        grad_out = lax.psum_scatter(grad_out, "batch", scatter_dimension=0, tiled=True)
        grad_vec = lax.psum(grad_vec, "batch")
    count, narrow = hidden // devices, width // devices
    grad_bias = lax.dynamic_slice(grad_vec[0], (index * count,), (count,))
    grad_norm = lax.dynamic_slice(grad_vec[:5], (0, hidden + index * narrow), (5, narrow))

    scale = (seqs * batch_parts * local * seq_parts) ** (-0.5)
    m_in, w_in_new, a_in = nesterov(
        weight_in, moment_in, average_in, grad_in.T, RATE_MATRIX, scale
    )
    m_out, w_out_new, a_out = nesterov(
        weight_out, moment_out, average_out, grad_out, RATE_MATRIX, scale
    )
    m_bias, b_new, a_bias = nesterov(
        bias_ff, moment_bias, average_bias, grad_bias, RATE_VECTOR, scale
    )
    m_norm, n_new, a_norm = nesterov(
        norm_vec, moment_norm, average_norm, grad_norm, RATE_VECTOR, scale
    )
    return (
        result.reshape(seqs, local, width),
        tokens_grad.reshape(seqs, local, width),
        m_in,
        w_in_new,
        a_in,
        m_out,
        w_out_new,
        a_out,
        m_bias,
        b_new,
        a_bias,
        m_norm,
        n_new,
        a_norm,
    )


def solution(mesh):
    tokens = P("batch", "seq", None)
    columns, rows, flat = P(None, ("seq", "batch")), P(("seq", "batch"), None), P(("seq", "batch"))
    return jax.shard_map(
        functools.partial(on_device, mesh.shape["seq"], mesh.shape["batch"]),
        mesh=mesh,
        in_specs=(tokens, tokens, columns, rows, flat, columns)
        + (columns, columns, rows, rows, flat, flat, columns, columns),
        out_specs=(tokens, tokens)
        + (columns,) * 3
        + (rows,) * 3
        + (flat,) * 3
        + (columns,) * 3,
        check_vma=False,
    )
```

```python
import functools
import math

import jax
import jax.numpy as jnp
import ml_dtypes
import numpy as np
from jax import lax
from jax.experimental import pallas as pl
from jax.experimental.pallas import tpu as pltpu
from jax.sharding import PartitionSpec as P

EPSILON = 1e-05
MOMENTUM = 0.9
AVG_DECAY = 0.9
RATE_MATRIX = 0.02
RATE_VECTOR = 0.1
LANES = 128
MESH = pl.DeviceIdType.MESH
F32 = jnp.float32
BF16 = jnp.bfloat16


class Sizes:
    def __init__(self, parts, batch_parts, seqs, local, width, hidden):
        self.parts = parts
        self.batch_parts = batch_parts
        self.seqs = seqs
        self.local = local
        self.width = width
        self.hidden = hidden
        self.length = local * parts
        self.per = width // parts
        self.per_pad = -(-self.per // 16) * 16
        self.rows = self.per_pad + 16
        self.group = max(1, 512 // local)
        self.groups = seqs // self.group
        self.glen = self.group * local
        self.half = local // 2
        self.pack = max(1, LANES // self.half)
        self.depth = parts * LANES
        self.pair = 2 if self.groups % 2 == 0 and self.depth <= 2048 else 1
        self.pairs = self.groups // self.pair
        self.lhs_rows = 2 * self.pair * self.group * self.rows
        self.shared = self.lhs_rows <= self.glen and self.depth <= hidden
        self.with_batch = batch_parts == 2
        self.seq_bits = parts.bit_length() - 1
        self.bits = self.seq_bits + (1 if self.with_batch else 0)
        self.shards = 1 << self.bits
        self.shard_rows = hidden // self.shards
        self.chunks = hidden // width
        self.chunk_shards = self.shards // self.chunks
        self.pieces = 3
        assert self.chunks <= 8 and self.shard_rows % (16 * self.pieces) == 0
        assert parts == 1 << self.seq_bits and self.half * self.pack == LANES
        assert self.group % self.pack == 0


def mixing_tables(z):
    width, per = z.width, z.per
    index = np.arange(width)
    angle = ((index[:, None] * index[None, :]) % width).astype(np.float32) * np.float32(
        2.0 * math.pi / width
    )
    cosine = np.cos(angle) / np.float32(math.sqrt(width))
    sine = np.sin(angle) / np.float32(math.sqrt(width))
    table = np.zeros((width + 16, width), np.float32)
    joined = np.zeros((width + 16, width), np.float32)
    for owner in range(z.parts):
        for slot in range(per):
            row, j = owner * per + slot, (owner // 2) * per + slot
            if owner % 2 == 0:
                table[row] = cosine[j]
                joined[row, j] = 1.0
                joined[row, (width - j) % width] = 1.0
            elif j > 0:
                table[row] = sine[j]
                joined[row, j] = -1.0
                joined[row, width - j] = 1.0
    table[width] = cosine[width // 2]
    joined[width, width // 2] = 1.0
    order = np.zeros((z.glen, z.glen), np.float32)
    row = 0
    for parity in range(2):
        for seq in range(z.group):
            for i in range(z.half):
                order[row, seq * z.local + 2 * i + parity] = 1.0
                row += 1
    low = ml_dtypes.bfloat16
    return table.astype(low), joined.astype(low), order.astype(low)


def sequence_tables(z):
    wave = (np.arange(z.length).astype(np.float32)) * np.float32(2.0 * math.pi / z.length)
    scale = np.float32(math.sqrt(z.length))
    waves = [
        (np.cos(wave) / scale).astype(ml_dtypes.bfloat16),
        (np.sin(wave) / scale).astype(ml_dtypes.bfloat16),
    ]
    source = np.arange(z.parts)[:, None, None] * z.local + 2 * np.arange(z.half)[None, None, :]
    source = np.broadcast_to(source, (z.parts, z.pack, z.half)).reshape(-1)
    out = np.arange(z.length // 2).reshape(z.parts // 2, z.local)
    result = np.empty((2, z.parts // 2, 2, z.depth, z.local), ml_dtypes.bfloat16)
    for parity in range(2):
        place = ((source + parity)[None, :, None] * out[:, None, :]) % z.length
        for kind in range(2):
            result[kind, :, parity] = waves[kind][place]
    return result


def dot(a, b):
    return jnp.dot(a, b, preferred_element_type=F32)


def dot_nt(a, b):
    return lax.dot_general(a, b, (((1,), (1,)), ((), ())), preferred_element_type=F32)


def dot_tn(a, b):
    return lax.dot_general(a, b, (((0,), (0,)), ((), ())), preferred_element_type=F32)


def normalize(value):
    center = value - jnp.mean(value, axis=-1, keepdims=True)
    spread = jnp.mean(center * center, axis=-1, keepdims=True)
    inverse = lax.rsqrt(spread + EPSILON)
    return center * inverse, inverse


def norm_backward(scaled, normed, inverse):
    return inverse * (
        scaled
        - jnp.mean(scaled, axis=-1, keepdims=True)
        - normed * jnp.mean(scaled * normed, axis=-1, keepdims=True)
    )


def gelu_and_slope(x):
    size = jnp.abs(x)
    t = 1.0 / (1.0 + (0.3275911 * math.sqrt(0.5)) * size)
    bell = jnp.exp(-0.5 * (x * x))
    poly = t * (
        0.5 * 0.254829592
        + t
        * (
            0.5 * -0.284496736
            + t * (0.5 * 1.421413741 + t * (0.5 * -1.453152027 + t * (0.5 * 1.061405429)))
        )
    )
    tail = poly * bell
    phi = jnp.where(x >= 0, 1.0 - tail, tail)
    return x * phi, phi + x * (bell * (1.0 / math.sqrt(2.0 * math.pi)))


STEPS = {"H": "hidden", "G": "gather", "T": "pair", "t": "single", "F": "feed", "S": "scatter", "E": "finish"}
KINDS = tuple(STEPS.values())


ORDER = (
    "G1", "H0", "G2", "H1", "G3", "t0", "H2", "H3", "G4", "t1", "G5",
    "F0", "T1", "F1", "F2", "T2", "F3", "S0", "t6", "S1", "S2", "t7",
    "E0", "S3", "E1", "E2", "S4", "E3", "S5",
)


def plan(z):
    if (z.groups, z.pairs, z.bits) == (4, 2, 5):
        return [(STEPS[name[0]], int(name[1:])) for name in ORDER]
    g = z.groups
    steps = [("hidden", i) for i in range(g)] + [("gather", i) for i in range(1, z.bits + 1)]
    steps += [("single", i) for i in range(g)] + [("feed", i) for i in range(g)]
    steps += [("scatter", 0)] + [("single", g + i) for i in range(g)]
    steps += [("scatter", i) for i in range(1, z.bits + 1)]
    return steps + [("finish", i) for i in range(g)]


def step_kernel(
    z,
    x_hbm,
    cot_hbm,
    shard_in,
    shard_out,
    shard_vec,
    seq_table,
    table,
    joined,
    order,
    result_hbm,
    grad_hbm,
    total_in,
    total_out,
    total_vec,
    landed,
    full,
    full_vec,
    sums,
    bias,
    vectors,
    vec_sum,
    vec_land,
    recv_a,
    recv_b,
    send,
    recv_sa,
    recv_sb,
    send_sa,
    send_sb,
    own_lhs,
    slots,
    source,
    cs,
    act,
    slope,
    normed_one,
    low,
    dlow,
    work,
    stage,
    inverse_one,
    sem_a,
    sem_b,
    sem_send,
    sem_sa,
    sem_sb,
    sem_ssa,
    sem_ssb,
    sem_gather_send,
    sem_gather_recv,
    sem_scatter_send,
    sem_scatter_recv,
    sem_local,
    sem_slot,
):
    parts, per, groups = z.parts, z.per, z.groups
    me = lax.axis_index("seq")
    core = lax.axis_index("batch")
    lhs = act if z.shared else own_lhs

    own = [lax.rem(lax.div(me, 1 << (z.seq_bits - 1 - d)), 2) for d in range(z.seq_bits)]
    own += [core] if z.with_batch else []
    weights = [1 << (z.bits - 1 - d) for d in range(z.bits)]
    middle = list(range(1, z.bits - 1))
    orders = [[0] + middle[r:] + middle[:r] + [z.bits - 1] for r in range(z.pieces)]
    piece_rows = z.shard_rows // z.pieces

    def piece(at, w):
        return full.at[:, at, pl.ds(w * piece_rows, piece_rows)]

    def partner(d):
        if d < z.seq_bits:
            return (me + (1 - 2 * own[d]) * (1 << (z.seq_bits - 1 - d)), core)
        return (me, 1 - core)

    def shard_at(free, k, flipped=None):
        index = 0
        for d in range(z.bits):
            if d in free:
                value = lax.rem(lax.div(k, 1 << free.index(d)), 2)
            elif d == flipped:
                value = 1 - own[d]
            else:
                value = own[d]
            index = index + value * weights[d]
        return index

    barrier = pltpu.get_barrier_semaphore()

    def greet(d, carry):
        pl.semaphore_signal(
            barrier, inc=1, device_id=(lax.rem(me + d, parts), core), device_id_type=MESH
        )
        return carry

    lax.fori_loop(1, parts, greet, 0)
    if z.with_batch:
        pl.semaphore_signal(barrier, inc=1, device_id=(me, 1 - core), device_id_type=MESH)
    greeted = parts - 1 + (1 if z.with_batch else 0)

    mine = shard_at((), 0)
    own_shards = [
        pltpu.make_async_copy(shard, place.at[mine], sem_local.at[w])
        for w, (shard, place) in enumerate(
            ((shard_in, full.at[0]), (shard_out, full.at[1]), (shard_vec, full_vec))
        )
    ]
    for copy in own_shards:
        copy.start()
    send_sa[...] = jnp.zeros_like(send_sa)
    vec_sum[...] = jnp.zeros_like(vec_sum)

    @pl.when(me != 0)
    def _():
        recv_sa[...] = jnp.zeros_like(recv_sa)

    pl.semaphore_wait(barrier, greeted)

    def gather_send(stage_no):
        for w in range(z.pieces + 1):
            path = orders[w % z.pieces]
            free, d = path[:stage_no], path[stage_no]

            def body(k, carry, w=w, free=free, d=d):
                at = shard_at(free, k)
                block = piece(at, w) if w < z.pieces else full_vec.at[at]
                pltpu.make_async_remote_copy(
                    src_ref=block,
                    dst_ref=block,
                    send_sem=sem_gather_send.at[w, stage_no],
                    recv_sem=sem_gather_recv.at[w, stage_no],
                    device_id=partner(d),
                    device_id_type=MESH,
                ).start()
                return carry

            lax.fori_loop(0, 1 << stage_no, body, 0)

    def gather_some(w, stage_no):
        if w < z.pieces:
            return landed.at[w, pl.ds(0, 1 << stage_no)]
        return full_vec.at[pl.ds(0, 1 << stage_no)]

    def gather_wait(stage_no):
        for w in range(z.pieces + 1):
            some = gather_some(w, stage_no)
            pltpu.make_async_copy(some, some, sem_gather_recv.at[w, stage_no]).wait()

    def gather_done():
        for stage_no in range(z.bits):
            for w in range(z.pieces + 1):
                some = gather_some(w, stage_no)
                pltpu.make_async_copy(some, some, sem_gather_send.at[w, stage_no]).wait()

    for copy in own_shards:
        copy.wait()
    gather_send(0)

    def gather_step(i):
        for stage_no in range(1, z.bits + 1):

            @pl.when(i == stage_no)
            def _(stage_no=stage_no):
                gather_wait(stage_no - 1)
                if stage_no < z.bits:
                    gather_send(stage_no)
                else:
                    gather_done()
                    place_vectors()

    def place_vectors():
        none = jnp.zeros((8, z.width - LANES), F32)
        lane = lax.broadcasted_iota(jnp.int32, (8, z.width), 1)
        wide = z.shard_rows
        narrow = z.width // z.shards
        for c in range(z.chunks):
            line = jnp.zeros((8, z.width), F32)
            for i in range(z.chunk_shards):
                row = jnp.concatenate([full_vec[c * z.chunk_shards + i, 0:8], none], axis=1)
                row = jnp.where(lane < wide, row, 0.0)
                line = line + (pltpu.roll(row, i * wide, 1) if i else row)
            bias[:, c * z.width : (c + 1) * z.width] = line[0:1]
        line = jnp.zeros((8, z.width), F32)
        for i in range(z.shards):
            row = jnp.concatenate([full_vec[i, 8:16], none], axis=1)
            row = jnp.where(lane < narrow, row, 0.0)
            line = line + (pltpu.roll(row, i * narrow, 1) if i else row)
        vectors[...] = line

    def wait_all(ref, sem):
        pltpu.make_async_copy(ref, ref, sem).wait()

    def wait_sent(g):
        some = send.at[g, pl.ds(0, parts - 1)]
        pltpu.make_async_copy(some, some, sem_send.at[g]).wait()

    def push(g, peer, landing, sem):
        @pl.when(peer != me)
        def _():
            pltpu.make_async_remote_copy(
                src_ref=send.at[g, peer],
                dst_ref=landing.at[g, me],
                send_sem=sem_send.at[g],
                recv_sem=sem.at[g],
                device_id=(peer, core),
                device_id_type=MESH,
            ).start()

        @pl.when(peer == me)
        def _():
            pltpu.make_async_copy(send.at[g, me], landing.at[g, me], sem.at[g]).start()

    def hidden_step(u):
        g = lax.rem(u, groups)
        tokens = pl.ds(pl.multiple_of(g * z.glen, z.glen), z.glen)

        @pl.when(u < groups)
        def _():
            copy = pltpu.make_async_copy(x_hbm.at[tokens], source, sem_local.at[3])
            copy.start()
            copy.wait()

        moved = dot(order[...], source[...]).astype(BF16)
        out = dot_nt(table[...], moved)

        @pl.when(u >= groups)
        def _():
            wait_sent(g)

            @pl.when(me != 0)
            def _():
                wait_all(send_sa.at[g], sem_ssa.at[g])

        send[g] = out[: z.width].reshape(parts, per, z.glen).astype(BF16)
        last = out[z.width : z.width + 1].astype(BF16).astype(F32)
        for r in range(z.glen // LANES):
            send_sa[g, r : r + 1, :] = last[:, r * LANES : (r + 1) * LANES]

        @pl.when(me != 0)
        def _():
            pltpu.make_async_remote_copy(
                src_ref=send_sa.at[g],
                dst_ref=recv_sa.at[g, me],
                send_sem=sem_ssa.at[g],
                recv_sem=sem_sa.at[g],
                device_id=(0, core),
                device_id_type=MESH,
            ).start()

        @pl.when(me == 0)
        def _():
            pltpu.make_async_copy(send_sa.at[g], recv_sa.at[g, 0], sem_sa.at[g]).start()

        def body(d, carry):
            push(g, lax.rem(me + d, parts), recv_a, sem_a)
            return carry

        lax.fori_loop(0, parts, body, 0)

    half_parts = parts // 2
    deep = z.depth // 2

    def fetch(j, quarter):
        return pltpu.make_async_copy(
            seq_table.at[
                lax.rem(me, 2),
                lax.rem(me + j, half_parts),
                quarter // 2,
                pl.ds(quarter % 2 * deep, deep),
            ],
            slots.at[quarter],
            sem_slot.at[quarter],
        )

    def pair_step(u):
        first = lax.rem(u, z.pairs) * z.pair
        sequence_transform([first + q for q in range(z.pair)], u >= z.pairs)

    def single_step(u):
        sequence_transform([lax.rem(u, groups)], u >= groups)

    def sequence_transform(members, returning):
        seqs = len(members) * z.group

        for q, g in enumerate(members):
            wait_all(recv_a.at[g], sem_a.at[g])

            @pl.when(me == 0)
            def _(g=g):
                wait_all(recv_sa.at[g], sem_sa.at[g])

            def gather_rows(c, carry, q=q, g=g):
                columns = pl.ds(pl.multiple_of(c * LANES, LANES), LANES)
                for parity in range(2):
                    for s in range(z.group):
                        at = parity * (z.group // z.pack) + s // z.pack
                        rows = recv_a[g, c, :, at * LANES : (at + 1) * LANES]
                        line = recv_sa[g, c, at : at + 1, :]
                        line = jnp.broadcast_to(line, (16, LANES)).astype(BF16)
                        if z.pack > 1:
                            lane = lax.broadcasted_iota(jnp.int32, (per, LANES), 1) // z.half
                            rows = jnp.where(lane == s % z.pack, rows.astype(F32), 0.0).astype(BF16)
                            lane = lax.broadcasted_iota(jnp.int32, (16, LANES), 1) // z.half
                            line = jnp.where(lane == s % z.pack, line.astype(F32), 0.0).astype(BF16)
                        base = (parity * seqs + q * z.group + s) * z.rows
                        lhs[base : base + per, columns] = rows
                        lhs[base + z.per_pad : base + z.rows, columns] = line
                return carry

            lax.fori_loop(0, parts, gather_rows, 0)
            wait_sent(g)

            @pl.when((me == 0) & returning)
            def _(g=g):
                some = send_sb.at[g, pl.ds(0, parts - 1)]
                pltpu.make_async_copy(some, some, sem_ssb.at[g]).wait()

        def push_both(g, peer):
            push(g, peer, recv_b, sem_b)

            @pl.when((me == 0) & (peer != 0))
            def _():
                pltpu.make_async_remote_copy(
                    src_ref=send_sb.at[g, peer],
                    dst_ref=recv_sb.at[g],
                    send_sem=sem_ssb.at[g],
                    recv_sem=sem_sb.at[g],
                    device_id=(peer, core),
                    device_id_type=MESH,
                ).start()

            @pl.when((me == 0) & (peer == 0))
            def _():
                pltpu.make_async_copy(send_sb.at[g, 0], recv_sb.at[g], sem_sb.at[g]).start()

        def body(j, carry):
            near = lax.rem(me + j, half_parts)
            halves = []
            for parity in range(2):
                total = 0.0
                for quarter in (2 * parity, 2 * parity + 1):
                    fetch(j, quarter).wait()
                    lanes = slice(quarter % 2 * deep, (quarter % 2 + 1) * deep)
                    rows = lhs[parity * seqs * z.rows : (parity + 1) * seqs * z.rows, lanes]
                    total = total + dot(rows, slots[quarter])

                    fetch(j + 1, quarter).start()

                halves.append(total.reshape(seqs, z.rows, z.local))

            even, odd = halves
            for peer, value in ((near, even + odd), (near + half_parts, even - odd)):
                for q, g in enumerate(members):
                    for s in range(z.group):
                        part = value[q * z.group + s]
                        lanes = slice(s * z.local, (s + 1) * z.local)
                        send[g, peer, :, lanes] = part[:per].astype(BF16)
                        for r in range(z.local // LANES):
                            at = s * (z.local // LANES) + r
                            send_sb[g, peer, at : at + 1, :] = part[
                                z.per_pad : z.per_pad + 1, r * LANES : (r + 1) * LANES
                            ]
                push_both(members[0], peer)
            return carry

        lax.fori_loop(0, half_parts, body, 0)
        for g in members[1:]:

            def later(d, carry, g=g):
                push_both(g, lax.rem(me + d, parts))
                return carry

            lax.fori_loop(0, parts, later, 0)

    def mixed(g):
        wait_all(recv_b.at[g], sem_b.at[g])
        wait_all(recv_sb.at[g], sem_sb.at[g])
        rows = recv_b[g]
        if per % 16:
            rows = rows.astype(F32).reshape(z.width, z.glen).astype(BF16)
        else:
            rows = rows.reshape(z.width, z.glen)
        line = jnp.concatenate([recv_sb[g, r : r + 1, :] for r in range(z.glen // LANES)], axis=1)
        line = jnp.broadcast_to(line, (16, z.glen)).astype(BF16)
        return dot_tn(rows, joined[: z.width]) + dot_tn(line, joined[z.width :])

    def tokens_of(g):
        return pl.ds(pl.multiple_of(g * z.glen, z.glen), z.glen)

    def feed_step(g):
        load_x = pltpu.make_async_copy(x_hbm.at[tokens_of(g)], source, sem_local.at[4])
        load_c = pltpu.make_async_copy(cot_hbm.at[tokens_of(g)], cs, sem_local.at[5])
        put_result = pltpu.make_async_copy(stage, result_hbm.at[tokens_of(g)], sem_local.at[6])
        put_grad = pltpu.make_async_copy(work, grad_hbm.at[tokens_of(g)], sem_local.at[7])
        load_x.start()
        load_c.start()
        value = mixed(g)
        load_x.wait()
        load_c.wait()
        normed, inverse = normalize(source[...].astype(F32) + value)
        normed_one[...] = normed
        inverse_one[...] = inverse
        low[...] = (normed * vectors[0:1, :] + vectors[1:2, :]).astype(BF16)
        work[...] = jnp.zeros_like(work)

        def forward(c, carry):
            lanes = pl.ds(pl.multiple_of(c * z.width, z.width), z.width)
            some = pl.ds(c * z.chunk_shards, z.chunk_shards)
            pre = dot_nt(low[...], full[0, some].reshape(z.width, z.width)) + bias[:, lanes]
            value, pull = gelu_and_slope(pre)
            value = value.astype(BF16)
            act[:, lanes] = value
            slope[:, lanes] = pull.astype(BF16)
            work[...] += dot(value, full[1, some].reshape(z.width, z.width))
            return carry

        lax.fori_loop(0, z.chunks, forward, 0, unroll=2)
        value = normed_one[...] * vectors[0:1, :] + vectors[1:2, :]
        normed, inverse = normalize(value + (work[...] + vectors[4:5, :]))
        stage[...] = normed * vectors[2:3, :] + vectors[3:4, :]
        put_result.start()
        grad = cs[...].astype(F32)
        vec_sum[10:11, :] += jnp.sum(grad * normed, axis=0, keepdims=True)
        vec_sum[11:12, :] += jnp.sum(grad, axis=0, keepdims=True)
        grad = norm_backward(grad * vectors[2:3, :], normed, inverse)
        work[...] = grad
        dffo = grad.astype(BF16)
        dlow[...] = dffo
        vec_sum[12:13, :] += jnp.sum(dffo.astype(F32), axis=0, keepdims=True)

        def backward(c, carry):
            lanes = pl.ds(pl.multiple_of(c * z.width, z.width), z.width)
            some = pl.ds(c * z.chunk_shards, z.chunk_shards)
            shape = (z.chunk_shards, z.shard_rows, z.width)
            dpre = dot_nt(dlow[...], full[1, some].reshape(z.width, z.width))
            dpre = (dpre * slope[:, lanes].astype(F32)).astype(BF16)
            vec_sum[pl.ds(c, 1), :] += jnp.sum(dpre.astype(F32), axis=0, keepdims=True)
            work[...] += dot(dpre, full[0, some].reshape(z.width, z.width))
            into_out = dot_tn(act[:, lanes], dlow[...]).reshape(shape)
            into_in = dot_tn(dpre, low[...]).reshape(shape)

            @pl.when(g == 0)
            def _():
                sums[1, some] = into_out
                sums[0, some] = into_in

            @pl.when(g > 0)
            def _():
                sums[1, some] += into_out
                sums[0, some] += into_in

            return carry

        lax.fori_loop(0, z.chunks, backward, 0)
        grad, normed = work[...], normed_one[...]
        vec_sum[8:9, :] += jnp.sum(grad * normed, axis=0, keepdims=True)
        vec_sum[9:10, :] += jnp.sum(grad, axis=0, keepdims=True)
        grad = norm_backward(grad * vectors[0:1, :], normed, inverse_one[...])
        source[...] = grad.astype(BF16)
        work[...] = grad
        put_grad.start()
        hidden_step(g + groups)
        put_result.wait()
        put_grad.wait()

    def finish_put(g):
        return pltpu.make_async_copy(stage, grad_hbm.at[tokens_of(g)], sem_local.at[6])

    def finish_step(g):
        load = pltpu.make_async_copy(grad_hbm.at[tokens_of(g)], work, sem_local.at[7])
        load.start()
        value = mixed(g)
        load.wait()

        @pl.when(g > 0)
        def _():
            finish_put(g - 1).wait()

        stage[...] = work[...] + value
        finish_put(g).start()

    offsets = [sum(1 << (z.bits - 1 - i) for i in range(s)) for s in range(z.bits)]

    def scatter_send(s):
        count = 1 << (z.bits - 1 - s)
        for w in range(z.pieces):
            path = orders[w][::-1]
            d, free = path[s], path[s + 1 :]

            def body(k, carry, w=w, d=d, free=free):
                at = shard_at(free, k, flipped=d)
                rows = pl.ds(w * piece_rows, piece_rows)
                full[:, at, rows] = sums[:, at, rows].astype(BF16)
                pltpu.make_async_remote_copy(
                    src_ref=piece(at, w),
                    dst_ref=landed.at[w, offsets[s] + k],
                    send_sem=sem_scatter_send.at[w, s],
                    recv_sem=sem_scatter_recv.at[w, s],
                    device_id=partner(d),
                    device_id_type=MESH,
                ).start()
                return carry

            lax.fori_loop(0, count, body, 0)
        pltpu.make_async_remote_copy(
            src_ref=vec_sum,
            dst_ref=vec_land.at[s],
            send_sem=sem_scatter_send.at[z.pieces, s],
            recv_sem=sem_scatter_recv.at[z.pieces, s],
            device_id=partner(orders[0][::-1][s]),
            device_id_type=MESH,
        ).start()

    def scatter_add(s):
        count = 1 << (z.bits - 1 - s)
        for w in range(z.pieces):
            free = orders[w][::-1][s + 1 :]
            some = landed.at[w, pl.ds(offsets[s], count)]
            wait_all(some, sem_scatter_recv.at[w, s])

            def fetch(k, carry, w=w, free=free):
                pltpu.make_async_copy(
                    landed.at[w, offsets[s] + k], piece(shard_at(free, k), w), sem_local.at[w]
                ).start()
                return carry

            lax.fori_loop(0, count, fetch, 0)
        wait_all(vec_sum, sem_scatter_send.at[z.pieces, s])
        wait_all(vec_land.at[s], sem_scatter_recv.at[z.pieces, s])
        vec_sum[...] += vec_land[s]
        for w in range(z.pieces):
            free = orders[w][::-1][s + 1 :]
            some = landed.at[w, pl.ds(offsets[s], count)]
            wait_all(some, sem_local.at[w])

            def add(k, carry, w=w, free=free):
                at, rows = shard_at(free, k), pl.ds(w * piece_rows, piece_rows)
                sums[:, at, rows] += full[:, at, rows].astype(F32)
                return carry

            lax.fori_loop(0, count, add, 0)

    def scatter_step(i):
        for s in range(z.bits + 1):

            @pl.when(i == s)
            def _(s=s):
                if s > 0:
                    scatter_add(s - 1)
                if s < z.bits:
                    scatter_send(s)

    steps = plan(z)
    bodies = (
        hidden_step,
        gather_step,
        pair_step,
        single_step,
        feed_step,
        scatter_step,
        finish_step,
    )
    used = {name for name, _ in steps}

    def one_step(s, carry):
        kind, argument = 0, 0
        for i, (name, value) in enumerate(steps):
            here = (s == i).astype(jnp.int32)
            kind = kind + here * KINDS.index(name)
            argument = argument + here * value
        for k, body in enumerate(bodies):
            if KINDS[k] not in used:
                continue

            @pl.when(kind == k)
            def _(body=body):
                body(argument)

        return carry

    for quarter in range(4):
        fetch(0, quarter).start()
    lax.fori_loop(0, len(steps), one_step, 0)
    for quarter in range(4):
        fetch(0, quarter).wait()

    for w, total in ((0, total_in), (1, total_out)):
        pltpu.make_async_copy(sums.at[w, mine], total, sem_local.at[w]).start()
    pltpu.make_async_copy(vec_sum, total_vec, sem_local.at[2]).start()
    finish_put(groups - 1).wait()
    for g in range(groups):
        wait_sent(g)

        @pl.when(me != 0)
        def _(g=g):
            wait_all(send_sa.at[g], sem_ssa.at[g])

        @pl.when(me == 0)
        def _(g=g):
            some = send_sb.at[g, pl.ds(0, parts - 1)]
            pltpu.make_async_copy(some, some, sem_ssb.at[g]).wait()

    for s in range(z.bits):
        for w in range(z.pieces):
            some = landed.at[w, pl.ds(offsets[s], 1 << (z.bits - 1 - s))]
            wait_all(some, sem_scatter_send.at[w, s])
    for w, total in ((0, total_in), (1, total_out)):
        pltpu.make_async_copy(sums.at[w, mine], total, sem_local.at[w]).wait()
    pltpu.make_async_copy(vec_sum, total_vec, sem_local.at[2]).wait()


def run_step(z, x, cot, shard_in, shard_out, shard_vec, tables):
    tokens = z.seqs * z.local
    shard = (2, z.shards, z.shard_rows, z.width)
    piece = (2, z.shard_rows // z.pieces, z.width)
    block = (z.glen, z.width)
    any_space, vmem = pl.BlockSpec(memory_space=pl.ANY), pl.BlockSpec(memory_space=pltpu.VMEM)
    dma = pltpu.SemaphoreType.DMA
    g = z.groups
    scratch = [
        pltpu.VMEM(shard, BF16),
        pltpu.VMEM((z.shards, 16, LANES), F32),
        pltpu.VMEM(shard, F32),
        pltpu.VMEM((1, z.hidden), F32),
        pltpu.VMEM((8, z.width), F32),
        pltpu.VMEM((16, z.width), F32),
        pltpu.VMEM((z.bits, 16, z.width), F32),
        pltpu.VMEM((g, z.parts, z.per, z.glen), BF16),
        pltpu.VMEM((g, z.parts, z.per, z.glen), BF16),
        pltpu.VMEM((g, z.parts, z.per, z.glen), BF16),
        pltpu.VMEM((g, z.parts, 8, LANES), F32),
        pltpu.VMEM((g, 8, LANES), F32),
        pltpu.VMEM((g, 8, LANES), F32),
        pltpu.VMEM((g, z.parts, 8, LANES), F32),
        pltpu.VMEM((16, LANES) if z.shared else (z.lhs_rows, z.depth), BF16),
        pltpu.VMEM((4, z.depth // 2, z.local), BF16),
        pltpu.VMEM((z.glen, z.width), BF16),
        pltpu.VMEM((z.glen, z.width), BF16),
        pltpu.VMEM((z.glen, z.hidden), BF16),
        pltpu.VMEM((z.glen, z.hidden), BF16),
        pltpu.VMEM(block, F32),
        pltpu.VMEM(block, BF16),
        pltpu.VMEM(block, BF16),
        pltpu.VMEM(block, F32),
        pltpu.VMEM(block, F32),
        pltpu.VMEM((z.glen, 1), F32),
        dma((g,)),
        dma((g,)),
        dma((g,)),
        dma((g,)),
        dma((g,)),
        dma((g,)),
        dma((g,)),
        dma((z.pieces + 1, z.bits)),
        dma((z.pieces + 1, z.bits)),
        dma((z.pieces + 1, z.bits)),
        dma((z.pieces + 1, z.bits)),
        dma((8,)),
        dma((4,)),
    ]
    return pl.pallas_call(
        functools.partial(step_kernel, z),
        out_shape=(
            jax.ShapeDtypeStruct((tokens, z.width), F32),
            jax.ShapeDtypeStruct((tokens, z.width), F32),
            jax.ShapeDtypeStruct(shard[2:], F32),
            jax.ShapeDtypeStruct(shard[2:], F32),
            jax.ShapeDtypeStruct((16, z.width), F32),
            jax.ShapeDtypeStruct((z.pieces, z.shards - 1) + piece, BF16),
        ),
        in_specs=[any_space] * 6 + [vmem] * 3,
        out_specs=(any_space,) * 6,
        scratch_shapes=scratch,
        compiler_params=pltpu.CompilerParams(
            collective_id=0, has_side_effects=True, vmem_limit_bytes=64 << 20
        ),
        cost_estimate=pl.CostEstimate(
            flops=12 * tokens * z.width * z.hidden + 16 * tokens * z.width * z.length // 16,
            bytes_accessed=40 * tokens * z.width,
            transcendentals=tokens * z.hidden,
        ),
    )(x, cot, shard_in, shard_out, shard_vec, *tables)


def nesterov(weight, moment, average, grad, rate, scale):
    scaled = grad * scale
    moment_new = MOMENTUM * moment + scaled
    weight_new = weight - rate * (scaled + MOMENTUM * moment_new)
    average_new = AVG_DECAY * average + (1.0 - AVG_DECAY) * weight_new
    return (moment_new, weight_new, average_new)


def on_device(
    seq_parts,
    batch_parts,
    layer_input_tokens,
    cotangent,
    weight_in,
    weight_out,
    bias_ff,
    norm_vec,
    moment_in,
    average_in,
    moment_out,
    average_out,
    moment_bias,
    average_bias,
    moment_norm,
    average_norm,
):
    seqs, local, width = layer_input_tokens.shape
    devices = seq_parts * batch_parts
    hidden = weight_out.shape[0] * devices
    z = Sizes(seq_parts, batch_parts, seqs, local, width, hidden)
    tokens = seqs * local

    shard_in = weight_in.T.astype(BF16)
    shard_out = weight_out.astype(BF16)
    bias_shard, norm_shard = bias_ff, norm_vec
    if not z.with_batch:
        shard_in, shard_out, bias_shard = (
            lax.all_gather(v, "batch", axis=0, tiled=True) for v in (shard_in, shard_out, bias_shard)
        )
        norm_shard = lax.all_gather(norm_shard, "batch", axis=1, tiled=True)
    bias_line = jnp.pad(bias_shard[None, :], ((0, 7), (0, LANES - bias_shard.shape[0])))
    norm_rows = jnp.pad(norm_shard, ((0, 3), (0, LANES - norm_shard.shape[1])))
    shard_vec = jnp.concatenate([bias_line, norm_rows], axis=0)

    tables = [jnp.asarray(sequence_tables(z))] + [jnp.asarray(t) for t in mixing_tables(z)]
    result, tokens_grad, grad_in, grad_out, grad_vec, _ = run_step(
        z,
        layer_input_tokens.reshape(tokens, width),
        cotangent.reshape(tokens, width),
        shard_in,
        shard_out,
        shard_vec,
        tables,
    )
    index = lax.axis_index("seq") * batch_parts + lax.axis_index("batch")
    if not z.with_batch:
        grad_in = lax.psum_scatter(grad_in, "batch", scatter_dimension=0, tiled=True)
        grad_out = lax.psum_scatter(grad_out, "batch", scatter_dimension=0, tiled=True)
        grad_vec = lax.psum(grad_vec, "batch")
    count, narrow = hidden // devices, width // devices
    grad_bias = lax.dynamic_slice(grad_vec[: z.chunks].reshape(hidden), (index * count,), (count,))
    grad_norm = lax.dynamic_slice(grad_vec[8:13], (0, index * narrow), (5, narrow))

    scale = (seqs * batch_parts * local * seq_parts) ** (-0.5)
    m_in, w_in_new, a_in = nesterov(
        weight_in, moment_in, average_in, grad_in.T, RATE_MATRIX, scale
    )
    m_out, w_out_new, a_out = nesterov(
        weight_out, moment_out, average_out, grad_out, RATE_MATRIX, scale
    )
    m_bias, b_new, a_bias = nesterov(
        bias_ff, moment_bias, average_bias, grad_bias, RATE_VECTOR, scale
    )
    m_norm, n_new, a_norm = nesterov(
        norm_vec, moment_norm, average_norm, grad_norm, RATE_VECTOR, scale
    )
    return (
        result.reshape(seqs, local, width),
        tokens_grad.reshape(seqs, local, width),
        m_in,
        w_in_new,
        a_in,
        m_out,
        w_out_new,
        a_out,
        m_bias,
        b_new,
        a_bias,
        m_norm,
        n_new,
        a_norm,
    )


def solution(mesh):
    tokens = P("batch", "seq", None)
    columns, rows, flat = P(None, ("seq", "batch")), P(("seq", "batch"), None), P(("seq", "batch"))
    return jax.shard_map(
        functools.partial(on_device, mesh.shape["seq"], mesh.shape["batch"]),
        mesh=mesh,
        in_specs=(tokens, tokens, columns, rows, flat, columns)
        + (columns, columns, rows, rows, flat, flat, columns, columns),
        out_specs=(tokens, tokens)
        + (columns,) * 3
        + (rows,) * 3
        + (flat,) * 3
        + (columns,) * 3,
        check_vma=False,
    )
```

```python
import functools
import math

import jax
import jax.numpy as jnp
import ml_dtypes
import numpy as np
from jax import lax
from jax.experimental import pallas as pl
from jax.experimental.pallas import tpu as pltpu
from jax.sharding import PartitionSpec as P

EPSILON = 1e-05
MOMENTUM = 0.9
AVG_DECAY = 0.9
RATE_MATRIX = 0.02
RATE_VECTOR = 0.1
LANES = 128
MESH = pl.DeviceIdType.MESH
F32 = jnp.float32
BF16 = jnp.bfloat16


class Sizes:
    def __init__(self, parts, batch_parts, seqs, local, width, hidden):
        self.parts = parts
        self.batch_parts = batch_parts
        self.seqs = seqs
        self.local = local
        self.width = width
        self.hidden = hidden
        self.length = local * parts
        self.per = width // parts
        self.per_pad = -(-self.per // 16) * 16
        self.rows = self.per_pad + 16
        self.group = max(1, 512 // local)
        self.groups = seqs // self.group
        self.glen = self.group * local
        self.half = local // 2
        self.pack = max(1, LANES // self.half)
        self.depth = parts * LANES
        self.pair = 2 if self.groups % 2 == 0 and self.depth <= 2048 else 1
        self.pairs = self.groups // self.pair
        self.lhs_rows = 2 * self.pair * self.group * self.rows
        self.shared = self.lhs_rows <= self.glen and self.depth <= hidden
        self.with_batch = batch_parts == 2
        self.seq_bits = parts.bit_length() - 1
        self.bits = self.seq_bits + (1 if self.with_batch else 0)
        self.shards = 1 << self.bits
        self.shard_rows = hidden // self.shards
        self.chunks = hidden // width
        self.chunk_shards = self.shards // self.chunks
        self.pieces = 3
        assert self.chunks <= 8 and self.shard_rows % (16 * self.pieces) == 0
        assert parts == 1 << self.seq_bits and self.half * self.pack == LANES
        assert self.group % self.pack == 0


def mixing_tables(z):
    width, per = z.width, z.per
    index = np.arange(width)
    angle = ((index[:, None] * index[None, :]) % width).astype(np.float32) * np.float32(
        2.0 * math.pi / width
    )
    cosine = np.cos(angle) / np.float32(math.sqrt(width))
    sine = np.sin(angle) / np.float32(math.sqrt(width))
    table = np.zeros((width + 16, width), np.float32)
    joined = np.zeros((width + 16, width), np.float32)
    for owner in range(z.parts):
        for slot in range(per):
            row, j = owner * per + slot, (owner // 2) * per + slot
            if owner % 2 == 0:
                table[row] = cosine[j]
                joined[row, j] = 1.0
                joined[row, (width - j) % width] = 1.0
            elif j > 0:
                table[row] = sine[j]
                joined[row, j] = -1.0
                joined[row, width - j] = 1.0
    table[width] = cosine[width // 2]
    joined[width, width // 2] = 1.0
    order = np.zeros((z.glen, z.glen), np.float32)
    row = 0
    for parity in range(2):
        for seq in range(z.group):
            for i in range(z.half):
                order[row, seq * z.local + 2 * i + parity] = 1.0
                row += 1
    low = ml_dtypes.bfloat16
    return table.astype(low), joined.astype(low), order.astype(low)


def sequence_tables(z):
    wave = (np.arange(z.length).astype(np.float32)) * np.float32(2.0 * math.pi / z.length)
    scale = np.float32(math.sqrt(z.length))
    waves = [
        (np.cos(wave) / scale).astype(ml_dtypes.bfloat16),
        (np.sin(wave) / scale).astype(ml_dtypes.bfloat16),
    ]
    source = np.arange(z.parts)[:, None, None] * z.local + 2 * np.arange(z.half)[None, None, :]
    source = np.broadcast_to(source, (z.parts, z.pack, z.half)).reshape(-1)
    out = np.arange(z.length // 2).reshape(z.parts // 2, z.local)
    result = np.empty((2, z.parts // 2, 2, z.depth, z.local), ml_dtypes.bfloat16)
    for parity in range(2):
        place = ((source + parity)[None, :, None] * out[:, None, :]) % z.length
        for kind in range(2):
            result[kind, :, parity] = waves[kind][place]
    return result


def dot(a, b):
    return jnp.dot(a, b, preferred_element_type=F32)


def dot_nt(a, b):
    return lax.dot_general(a, b, (((1,), (1,)), ((), ())), preferred_element_type=F32)


def dot_tn(a, b):
    return lax.dot_general(a, b, (((0,), (0,)), ((), ())), preferred_element_type=F32)


def normalize(value):
    center = value - jnp.mean(value, axis=-1, keepdims=True)
    spread = jnp.mean(center * center, axis=-1, keepdims=True)
    inverse = lax.rsqrt(spread + EPSILON)
    return center * inverse, inverse


def norm_backward(scaled, normed, inverse):
    return inverse * (
        scaled
        - jnp.mean(scaled, axis=-1, keepdims=True)
        - normed * jnp.mean(scaled * normed, axis=-1, keepdims=True)
    )


def gelu_and_slope(x):
    size = jnp.abs(x)
    t = 1.0 / (1.0 + (0.3275911 * math.sqrt(0.5)) * size)
    bell = jnp.exp(-0.5 * (x * x))
    poly = t * (
        0.5 * 0.254829592
        + t
        * (
            0.5 * -0.284496736
            + t * (0.5 * 1.421413741 + t * (0.5 * -1.453152027 + t * (0.5 * 1.061405429)))
        )
    )
    tail = poly * bell
    phi = jnp.where(x >= 0, 1.0 - tail, tail)
    return x * phi, phi + x * (bell * (1.0 / math.sqrt(2.0 * math.pi)))


STEPS = {"H": "hidden", "G": "gather", "T": "pair", "t": "single", "F": "feed", "S": "scatter", "E": "finish"}
KINDS = tuple(STEPS.values())


ORDER = (
    "G1", "H0", "G2", "H1", "G3", "t0", "H2", "H3", "G4", "t1", "G5",
    "F0", "T1", "F1", "F2", "T2", "F3", "S0", "S1", "t6", "S2", "t7",
    "E0", "S3", "E1", "E2", "S4", "E3", "S5",
)


def plan(z):
    if (z.groups, z.pairs, z.bits) == (4, 2, 5):
        return [(STEPS[name[0]], int(name[1:])) for name in ORDER]
    g = z.groups
    steps = [("hidden", i) for i in range(g)] + [("gather", i) for i in range(1, z.bits + 1)]
    steps += [("single", i) for i in range(g)] + [("feed", i) for i in range(g)]
    steps += [("scatter", 0)] + [("single", g + i) for i in range(g)]
    steps += [("scatter", i) for i in range(1, z.bits + 1)]
    return steps + [("finish", i) for i in range(g)]


def step_kernel(
    z,
    x_hbm,
    cot_hbm,
    shard_in,
    shard_out,
    shard_vec,
    seq_table,
    table_hbm,
    joined_hbm,
    order_hbm,
    result_hbm,
    grad_hbm,
    total_in,
    total_out,
    total_vec,
    landed,
    full,
    full_vec,
    sums,
    bias,
    vectors,
    vec_sum,
    vec_land,
    recv_a,
    recv_b,
    send,
    recv_sa,
    recv_sb,
    send_sa,
    send_sb,
    own_lhs,
    slots,
    source,
    cs,
    act,
    slope,
    normed_one,
    low,
    dlow,
    work,
    stage,
    inverse_one,
    table,
    joined,
    order,
    sem_a,
    sem_b,
    sem_send,
    sem_sa,
    sem_sb,
    sem_ssa,
    sem_ssb,
    sem_gather_send,
    sem_gather_recv,
    sem_scatter_send,
    sem_scatter_recv,
    sem_local,
    sem_slot,
    sem_table,
):
    parts, per, groups = z.parts, z.per, z.groups
    me = lax.axis_index("seq")
    core = lax.axis_index("batch")
    lhs = act if z.shared else own_lhs

    own = [lax.rem(lax.div(me, 1 << (z.seq_bits - 1 - d)), 2) for d in range(z.seq_bits)]
    own += [core] if z.with_batch else []
    weights = [1 << (z.bits - 1 - d) for d in range(z.bits)]
    middle = list(range(1, z.bits - 1))
    orders = [[0] + middle[r:] + middle[:r] + [z.bits - 1] for r in range(z.pieces)]
    piece_rows = z.shard_rows // z.pieces

    def piece(at, w):
        return full.at[:, at, pl.ds(w * piece_rows, piece_rows)]

    def partner(d):
        if d < z.seq_bits:
            return (me + (1 - 2 * own[d]) * (1 << (z.seq_bits - 1 - d)), core)
        return (me, 1 - core)

    def shard_at(free, k, flipped=None):
        index = 0
        for d in range(z.bits):
            if d in free:
                value = lax.rem(lax.div(k, 1 << free.index(d)), 2)
            elif d == flipped:
                value = 1 - own[d]
            else:
                value = own[d]
            index = index + value * weights[d]
        return index

    barrier = pltpu.get_barrier_semaphore()

    def greet(d, carry):
        pl.semaphore_signal(
            barrier, inc=1, device_id=(lax.rem(me + d, parts), core), device_id_type=MESH
        )
        return carry

    lax.fori_loop(1, parts, greet, 0)
    if z.with_batch:
        pl.semaphore_signal(barrier, inc=1, device_id=(me, 1 - core), device_id_type=MESH)
    greeted = parts - 1 + (1 if z.with_batch else 0)

    loads = [
        pltpu.make_async_copy(there, here, sem_table.at[n])
        for n, (there, here) in enumerate(
            ((table_hbm, table), (joined_hbm, joined), (order_hbm, order))
        )
    ]
    for copy in loads:
        copy.start()
    mine = shard_at((), 0)
    own_shards = [
        pltpu.make_async_copy(shard, place.at[mine], sem_local.at[w])
        for w, (shard, place) in enumerate(
            ((shard_in, full.at[0]), (shard_out, full.at[1]), (shard_vec, full_vec))
        )
    ]
    if z.with_batch:
        rough = work.at[pl.ds(0, z.shard_rows)]
        own_shards[1] = pltpu.make_async_copy(shard_out, rough, sem_local.at[1])
    for copy in own_shards:
        copy.start()
    send_sa[...] = jnp.zeros_like(send_sa)
    vec_sum[...] = jnp.zeros_like(vec_sum)

    @pl.when(me != 0)
    def _():
        recv_sa[...] = jnp.zeros_like(recv_sa)

    pl.semaphore_wait(barrier, greeted)

    def gather_send(stage_no):
        for w in range(z.pieces + 1):
            path = orders[w % z.pieces]
            free, d = path[:stage_no], path[stage_no]

            def body(k, carry, w=w, free=free, d=d):
                at = shard_at(free, k)
                block = piece(at, w) if w < z.pieces else full_vec.at[at]
                pltpu.make_async_remote_copy(
                    src_ref=block,
                    dst_ref=block,
                    send_sem=sem_gather_send.at[w, stage_no],
                    recv_sem=sem_gather_recv.at[w, stage_no],
                    device_id=partner(d),
                    device_id_type=MESH,
                ).start()
                return carry

            lax.fori_loop(0, 1 << stage_no, body, 0)

    def gather_some(w, stage_no):
        if w < z.pieces:
            return landed.at[w, pl.ds(0, 1 << stage_no)]
        return full_vec.at[pl.ds(0, 1 << stage_no)]

    def gather_wait(stage_no):
        for w in range(z.pieces + 1):
            some = gather_some(w, stage_no)
            pltpu.make_async_copy(some, some, sem_gather_recv.at[w, stage_no]).wait()

    def gather_done():
        for stage_no in range(z.bits):
            for w in range(z.pieces + 1):
                some = gather_some(w, stage_no)
                pltpu.make_async_copy(some, some, sem_gather_send.at[w, stage_no]).wait()

    for copy in own_shards:
        copy.wait()
    if z.with_batch:
        full[1, mine] = work[0 : z.shard_rows, :].astype(BF16)
    gather_send(0)

    def gather_step(i):
        for stage_no in range(1, z.bits + 1):

            @pl.when(i == stage_no)
            def _(stage_no=stage_no):
                gather_wait(stage_no - 1)
                if stage_no < z.bits:
                    gather_send(stage_no)
                else:
                    gather_done()
                    place_vectors()

    def place_vectors():
        none = jnp.zeros((8, z.width - LANES), F32)
        lane = lax.broadcasted_iota(jnp.int32, (8, z.width), 1)
        wide = z.shard_rows
        narrow = z.width // z.shards
        for c in range(z.chunks):
            line = jnp.zeros((8, z.width), F32)
            for i in range(z.chunk_shards):
                row = jnp.concatenate([full_vec[c * z.chunk_shards + i, 0:8], none], axis=1)
                row = jnp.where(lane < wide, row, 0.0)
                line = line + (pltpu.roll(row, i * wide, 1) if i else row)
            bias[:, c * z.width : (c + 1) * z.width] = line[0:1]
        line = jnp.zeros((8, z.width), F32)
        for i in range(z.shards):
            row = jnp.concatenate([full_vec[i, 8:16], none], axis=1)
            row = jnp.where(lane < narrow, row, 0.0)
            line = line + (pltpu.roll(row, i * narrow, 1) if i else row)
        vectors[...] = line

    def wait_all(ref, sem):
        pltpu.make_async_copy(ref, ref, sem).wait()

    def wait_sent(g):
        some = send.at[g, pl.ds(0, parts - 1)]
        pltpu.make_async_copy(some, some, sem_send.at[g]).wait()

    def push(g, peer, landing, sem):
        @pl.when(peer != me)
        def _():
            pltpu.make_async_remote_copy(
                src_ref=send.at[g, peer],
                dst_ref=landing.at[g, me],
                send_sem=sem_send.at[g],
                recv_sem=sem.at[g],
                device_id=(peer, core),
                device_id_type=MESH,
            ).start()

        @pl.when(peer == me)
        def _():
            pltpu.make_async_copy(send.at[g, me], landing.at[g, me], sem.at[g]).start()

    def hidden_step(u):
        g = lax.rem(u, groups)
        tokens = pl.ds(pl.multiple_of(g * z.glen, z.glen), z.glen)

        @pl.when(u < groups)
        def _():
            copy = pltpu.make_async_copy(x_hbm.at[tokens], source, sem_local.at[3])
            copy.start()
            copy.wait()

        moved = dot(order[...], source[...]).astype(BF16)
        out = dot_nt(table[...], moved)

        @pl.when(u >= groups)
        def _():
            wait_sent(g)

            @pl.when(me != 0)
            def _():
                wait_all(send_sa.at[g], sem_ssa.at[g])

        send[g] = out[: z.width].reshape(parts, per, z.glen).astype(BF16)
        last = out[z.width : z.width + 1].astype(BF16).astype(F32)
        for r in range(z.glen // LANES):
            send_sa[g, r : r + 1, :] = last[:, r * LANES : (r + 1) * LANES]

        @pl.when(me != 0)
        def _():
            pltpu.make_async_remote_copy(
                src_ref=send_sa.at[g],
                dst_ref=recv_sa.at[g, me],
                send_sem=sem_ssa.at[g],
                recv_sem=sem_sa.at[g],
                device_id=(0, core),
                device_id_type=MESH,
            ).start()

        @pl.when(me == 0)
        def _():
            pltpu.make_async_copy(send_sa.at[g], recv_sa.at[g, 0], sem_sa.at[g]).start()

        def body(d, carry):
            push(g, lax.rem(me + d, parts), recv_a, sem_a)
            return carry

        lax.fori_loop(0, parts, body, 0)

    half_parts = parts // 2
    deep = z.depth // 2

    def fetch(j, quarter):
        return pltpu.make_async_copy(
            seq_table.at[
                lax.rem(me, 2),
                lax.rem(me + j, half_parts),
                quarter // 2,
                pl.ds(quarter % 2 * deep, deep),
            ],
            slots.at[quarter],
            sem_slot.at[quarter],
        )

    def pair_step(u):
        first = lax.rem(u, z.pairs) * z.pair
        sequence_transform([first + q for q in range(z.pair)], u >= z.pairs)

    def single_step(u):
        sequence_transform([lax.rem(u, groups)], u >= groups)

    def sequence_transform(members, returning):
        seqs = len(members) * z.group

        for q, g in enumerate(members):
            wait_all(recv_a.at[g], sem_a.at[g])

            @pl.when(me == 0)
            def _(g=g):
                wait_all(recv_sa.at[g], sem_sa.at[g])

            def gather_rows(c, carry, q=q, g=g):
                columns = pl.ds(pl.multiple_of(c * LANES, LANES), LANES)
                for parity in range(2):
                    for s in range(z.group):
                        at = parity * (z.group // z.pack) + s // z.pack
                        rows = recv_a[g, c, :, at * LANES : (at + 1) * LANES]
                        line = recv_sa[g, c, at : at + 1, :]
                        line = jnp.broadcast_to(line, (16, LANES)).astype(BF16)
                        if z.pack > 1:
                            lane = lax.broadcasted_iota(jnp.int32, (per, LANES), 1) // z.half
                            rows = jnp.where(lane == s % z.pack, rows.astype(F32), 0.0).astype(BF16)
                            lane = lax.broadcasted_iota(jnp.int32, (16, LANES), 1) // z.half
                            line = jnp.where(lane == s % z.pack, line.astype(F32), 0.0).astype(BF16)
                        base = (parity * seqs + q * z.group + s) * z.rows
                        lhs[base : base + per, columns] = rows
                        lhs[base + z.per_pad : base + z.rows, columns] = line
                return carry

            lax.fori_loop(0, parts, gather_rows, 0)
            wait_sent(g)

            @pl.when((me == 0) & returning)
            def _(g=g):
                some = send_sb.at[g, pl.ds(0, parts - 1)]
                pltpu.make_async_copy(some, some, sem_ssb.at[g]).wait()

        def push_both(g, peer):
            push(g, peer, recv_b, sem_b)

            @pl.when((me == 0) & (peer != 0))
            def _():
                pltpu.make_async_remote_copy(
                    src_ref=send_sb.at[g, peer],
                    dst_ref=recv_sb.at[g],
                    send_sem=sem_ssb.at[g],
                    recv_sem=sem_sb.at[g],
                    device_id=(peer, core),
                    device_id_type=MESH,
                ).start()

            @pl.when((me == 0) & (peer == 0))
            def _():
                pltpu.make_async_copy(send_sb.at[g, 0], recv_sb.at[g], sem_sb.at[g]).start()

        def body(j, carry):
            near = lax.rem(me + j, half_parts)
            halves = []
            for parity in range(2):
                total = 0.0
                for quarter in (2 * parity, 2 * parity + 1):
                    fetch(j, quarter).wait()
                    lanes = slice(quarter % 2 * deep, (quarter % 2 + 1) * deep)
                    rows = lhs[parity * seqs * z.rows : (parity + 1) * seqs * z.rows, lanes]
                    total = total + dot(rows, slots[quarter])

                    fetch(j + 1, quarter).start()

                halves.append(total.reshape(seqs, z.rows, z.local))

            even, odd = halves
            for peer, value in ((near, even + odd), (near + half_parts, even - odd)):
                for q, g in enumerate(members):
                    for s in range(z.group):
                        part = value[q * z.group + s]
                        lanes = slice(s * z.local, (s + 1) * z.local)
                        send[g, peer, :, lanes] = part[:per].astype(BF16)
                        for r in range(z.local // LANES):
                            at = s * (z.local // LANES) + r
                            send_sb[g, peer, at : at + 1, :] = part[
                                z.per_pad : z.per_pad + 1, r * LANES : (r + 1) * LANES
                            ]
                push_both(members[0], peer)
            return carry

        lax.fori_loop(0, half_parts, body, 0)
        for g in members[1:]:

            def later(d, carry, g=g):
                push_both(g, lax.rem(me + d, parts))
                return carry

            lax.fori_loop(0, parts, later, 0)

    def mixed(g):
        wait_all(recv_b.at[g], sem_b.at[g])
        wait_all(recv_sb.at[g], sem_sb.at[g])
        rows = recv_b[g]
        if per % 16:
            rows = rows.astype(F32).reshape(z.width, z.glen).astype(BF16)
        else:
            rows = rows.reshape(z.width, z.glen)
        line = jnp.concatenate([recv_sb[g, r : r + 1, :] for r in range(z.glen // LANES)], axis=1)
        line = jnp.broadcast_to(line, (16, z.glen)).astype(BF16)
        return dot_tn(rows, joined[: z.width]) + dot_tn(line, joined[z.width :])

    def tokens_of(g):
        return pl.ds(pl.multiple_of(g * z.glen, z.glen), z.glen)

    def feed_step(g):
        load_x = pltpu.make_async_copy(x_hbm.at[tokens_of(g)], source, sem_local.at[4])
        load_c = pltpu.make_async_copy(cot_hbm.at[tokens_of(g)], cs, sem_local.at[5])
        put_result = pltpu.make_async_copy(stage, result_hbm.at[tokens_of(g)], sem_local.at[6])
        put_grad = pltpu.make_async_copy(work, grad_hbm.at[tokens_of(g)], sem_local.at[7])
        load_x.start()
        load_c.start()
        value = mixed(g)
        load_x.wait()
        load_c.wait()
        normed, inverse = normalize(source[...].astype(F32) + value)
        normed_one[...] = normed
        inverse_one[...] = inverse
        low[...] = (normed * vectors[0:1, :] + vectors[1:2, :]).astype(BF16)
        work[...] = jnp.zeros_like(work)

        def forward(c, carry):
            lanes = pl.ds(pl.multiple_of(c * z.width, z.width), z.width)
            some = pl.ds(c * z.chunk_shards, z.chunk_shards)
            pre = dot_nt(low[...], full[0, some].reshape(z.width, z.width)) + bias[:, lanes]
            value, pull = gelu_and_slope(pre)
            value = value.astype(BF16)
            act[:, lanes] = value
            slope[:, lanes] = pull.astype(BF16)
            work[...] += dot(value, full[1, some].reshape(z.width, z.width))
            return carry

        lax.fori_loop(0, z.chunks, forward, 0, unroll=2)
        value = normed_one[...] * vectors[0:1, :] + vectors[1:2, :]
        normed, inverse = normalize(value + (work[...] + vectors[4:5, :]))
        stage[...] = normed * vectors[2:3, :] + vectors[3:4, :]
        put_result.start()
        grad = cs[...].astype(F32)
        vec_sum[10:11, :] += jnp.sum(grad * normed, axis=0, keepdims=True)
        vec_sum[11:12, :] += jnp.sum(grad, axis=0, keepdims=True)
        grad = norm_backward(grad * vectors[2:3, :], normed, inverse)
        work[...] = grad
        dffo = grad.astype(BF16)
        dlow[...] = dffo
        vec_sum[12:13, :] += jnp.sum(dffo.astype(F32), axis=0, keepdims=True)

        def backward(c, carry):
            lanes = pl.ds(pl.multiple_of(c * z.width, z.width), z.width)
            some = pl.ds(c * z.chunk_shards, z.chunk_shards)
            shape = (z.chunk_shards, z.shard_rows, z.width)
            dpre = dot_nt(dlow[...], full[1, some].reshape(z.width, z.width))
            dpre = (dpre * slope[:, lanes].astype(F32)).astype(BF16)
            vec_sum[pl.ds(c, 1), :] += jnp.sum(dpre.astype(F32), axis=0, keepdims=True)
            work[...] += dot(dpre, full[0, some].reshape(z.width, z.width))
            into_out = dot_tn(act[:, lanes], dlow[...]).reshape(shape)
            into_in = dot_tn(dpre, low[...]).reshape(shape)

            @pl.when(g == 0)
            def _():
                sums[1, some] = into_out
                sums[0, some] = into_in

            @pl.when(g > 0)
            def _():
                sums[1, some] += into_out
                sums[0, some] += into_in

            @pl.when(g == groups - 1)
            def _():
                scatter_first(c)

            return carry

        lax.fori_loop(0, z.chunks, backward, 0)
        grad, normed = work[...], normed_one[...]
        vec_sum[8:9, :] += jnp.sum(grad * normed, axis=0, keepdims=True)
        vec_sum[9:10, :] += jnp.sum(grad, axis=0, keepdims=True)
        grad = norm_backward(grad * vectors[0:1, :], normed, inverse_one[...])
        source[...] = grad.astype(BF16)
        work[...] = grad
        put_grad.start()
        hidden_step(g + groups)
        put_result.wait()
        put_grad.wait()

    def finish_put(g):
        return pltpu.make_async_copy(stage, grad_hbm.at[tokens_of(g)], sem_local.at[6])

    def finish_step(g):
        load = pltpu.make_async_copy(grad_hbm.at[tokens_of(g)], work, sem_local.at[7])
        load.start()
        value = mixed(g)
        load.wait()

        @pl.when(g > 0)
        def _():
            finish_put(g - 1).wait()

        stage[...] = work[...] + value
        finish_put(g).start()

    offsets = [sum(1 << (z.bits - 1 - i) for i in range(s)) for s in range(z.bits)]

    def scatter_block(s, w, k, at, d):
        rows = pl.ds(w * piece_rows, piece_rows)
        full[:, at, rows] = sums[:, at, rows].astype(BF16)
        pltpu.make_async_remote_copy(
            src_ref=piece(at, w),
            dst_ref=landed.at[w, offsets[s] + k],
            send_sem=sem_scatter_send.at[w, s],
            recv_sem=sem_scatter_recv.at[w, s],
            device_id=partner(d),
            device_id_type=MESH,
        ).start()

    def scatter_first(c):
        d = z.bits - 1

        def body(i, carry):
            at = c * z.chunk_shards + 2 * i + 1 - own[d]
            for w in range(z.pieces):
                free = orders[w][::-1][1:]
                k = 0
                for n, e in enumerate(free):
                    k = k + lax.rem(lax.div(at, weights[e]), 2) * (1 << n)
                scatter_block(0, w, k, at, d)
            return carry

        lax.fori_loop(0, z.chunk_shards // 2, body, 0)

    def scatter_send(s):
        count = 1 << (z.bits - 1 - s)
        for w in range(z.pieces if s > 0 else 0):
            path = orders[w][::-1]
            d, free = path[s], path[s + 1 :]

            def body(k, carry, w=w, d=d, free=free):
                scatter_block(s, w, k, shard_at(free, k, flipped=d), d)
                return carry

            lax.fori_loop(0, count, body, 0)
        pltpu.make_async_remote_copy(
            src_ref=vec_sum,
            dst_ref=vec_land.at[s],
            send_sem=sem_scatter_send.at[z.pieces, s],
            recv_sem=sem_scatter_recv.at[z.pieces, s],
            device_id=partner(orders[0][::-1][s]),
            device_id_type=MESH,
        ).start()

    def scatter_add(s):
        count = 1 << (z.bits - 1 - s)
        for w in range(z.pieces):
            free = orders[w][::-1][s + 1 :]
            some = landed.at[w, pl.ds(offsets[s], count)]
            wait_all(some, sem_scatter_recv.at[w, s])

            def fetch(k, carry, w=w, free=free):
                pltpu.make_async_copy(
                    landed.at[w, offsets[s] + k], piece(shard_at(free, k), w), sem_local.at[w]
                ).start()
                return carry

            lax.fori_loop(0, count, fetch, 0)
        wait_all(vec_sum, sem_scatter_send.at[z.pieces, s])
        wait_all(vec_land.at[s], sem_scatter_recv.at[z.pieces, s])
        vec_sum[...] += vec_land[s]
        for w in range(z.pieces):
            free = orders[w][::-1][s + 1 :]
            some = landed.at[w, pl.ds(offsets[s], count)]
            wait_all(some, sem_local.at[w])

            def add(k, carry, w=w, free=free):
                at, rows = shard_at(free, k), pl.ds(w * piece_rows, piece_rows)
                sums[:, at, rows] += full[:, at, rows].astype(F32)
                return carry

            lax.fori_loop(0, count, add, 0)

    def scatter_step(i):
        for s in range(z.bits + 1):

            @pl.when(i == s)
            def _(s=s):
                if s > 0:
                    scatter_add(s - 1)
                if s < z.bits:
                    scatter_send(s)

    steps = plan(z)
    bodies = (
        hidden_step,
        gather_step,
        pair_step,
        single_step,
        feed_step,
        scatter_step,
        finish_step,
    )
    used = {name for name, _ in steps}

    def one_step(s, carry):
        kind, argument = 0, 0
        for i, (name, value) in enumerate(steps):
            here = (s == i).astype(jnp.int32)
            kind = kind + here * KINDS.index(name)
            argument = argument + here * value
        for k, body in enumerate(bodies):
            if KINDS[k] not in used:
                continue

            @pl.when(kind == k)
            def _(body=body):
                body(argument)

        return carry

    for copy in loads:
        copy.wait()
    for quarter in range(4):
        fetch(0, quarter).start()
    lax.fori_loop(0, len(steps), one_step, 0)
    for quarter in range(4):
        fetch(0, quarter).wait()

    for w, total in ((0, total_in), (1, total_out)):
        pltpu.make_async_copy(sums.at[w, mine], total, sem_local.at[w]).start()
    pltpu.make_async_copy(vec_sum, total_vec, sem_local.at[2]).start()
    finish_put(groups - 1).wait()
    for g in range(groups):
        wait_sent(g)

        @pl.when(me != 0)
        def _(g=g):
            wait_all(send_sa.at[g], sem_ssa.at[g])

        @pl.when(me == 0)
        def _(g=g):
            some = send_sb.at[g, pl.ds(0, parts - 1)]
            pltpu.make_async_copy(some, some, sem_ssb.at[g]).wait()

    for s in range(z.bits):
        for w in range(z.pieces):
            some = landed.at[w, pl.ds(offsets[s], 1 << (z.bits - 1 - s))]
            wait_all(some, sem_scatter_send.at[w, s])
    for w, total in ((0, total_in), (1, total_out)):
        pltpu.make_async_copy(sums.at[w, mine], total, sem_local.at[w]).wait()
    pltpu.make_async_copy(vec_sum, total_vec, sem_local.at[2]).wait()


def run_step(z, x, cot, shard_in, shard_out, shard_vec, tables):
    tokens = z.seqs * z.local
    shard = (2, z.shards, z.shard_rows, z.width)
    piece = (2, z.shard_rows // z.pieces, z.width)
    block = (z.glen, z.width)
    any_space = pl.BlockSpec(memory_space=pl.ANY)
    dma = pltpu.SemaphoreType.DMA
    g = z.groups
    scratch = [
        pltpu.VMEM(shard, BF16),
        pltpu.VMEM((z.shards, 16, LANES), F32),
        pltpu.VMEM(shard, F32),
        pltpu.VMEM((1, z.hidden), F32),
        pltpu.VMEM((8, z.width), F32),
        pltpu.VMEM((16, z.width), F32),
        pltpu.VMEM((z.bits, 16, z.width), F32),
        pltpu.VMEM((g, z.parts, z.per, z.glen), BF16),
        pltpu.VMEM((g, z.parts, z.per, z.glen), BF16),
        pltpu.VMEM((g, z.parts, z.per, z.glen), BF16),
        pltpu.VMEM((g, z.parts, 8, LANES), F32),
        pltpu.VMEM((g, 8, LANES), F32),
        pltpu.VMEM((g, 8, LANES), F32),
        pltpu.VMEM((g, z.parts, 8, LANES), F32),
        pltpu.VMEM((16, LANES) if z.shared else (z.lhs_rows, z.depth), BF16),
        pltpu.VMEM((4, z.depth // 2, z.local), BF16),
        pltpu.VMEM((z.glen, z.width), BF16),
        pltpu.VMEM((z.glen, z.width), BF16),
        pltpu.VMEM((z.glen, z.hidden), BF16),
        pltpu.VMEM((z.glen, z.hidden), BF16),
        pltpu.VMEM(block, F32),
        pltpu.VMEM(block, BF16),
        pltpu.VMEM(block, BF16),
        pltpu.VMEM(block, F32),
        pltpu.VMEM(block, F32),
        pltpu.VMEM((z.glen, 1), F32),
        pltpu.VMEM((z.width + 16, z.width), BF16),
        pltpu.VMEM((z.width + 16, z.width), BF16),
        pltpu.VMEM((z.glen, z.glen), BF16),
        dma((g,)),
        dma((g,)),
        dma((g,)),
        dma((g,)),
        dma((g,)),
        dma((g,)),
        dma((g,)),
        dma((z.pieces + 1, z.bits)),
        dma((z.pieces + 1, z.bits)),
        dma((z.pieces + 1, z.bits)),
        dma((z.pieces + 1, z.bits)),
        dma((8,)),
        dma((4,)),
        dma((3,)),
    ]
    return pl.pallas_call(
        functools.partial(step_kernel, z),
        out_shape=(
            jax.ShapeDtypeStruct((tokens, z.width), F32),
            jax.ShapeDtypeStruct((tokens, z.width), F32),
            jax.ShapeDtypeStruct(shard[2:], F32),
            jax.ShapeDtypeStruct(shard[2:], F32),
            jax.ShapeDtypeStruct((16, z.width), F32),
            jax.ShapeDtypeStruct((z.pieces, z.shards - 1) + piece, BF16),
        ),
        in_specs=[any_space] * 9,
        out_specs=(any_space,) * 6,
        scratch_shapes=scratch,
        compiler_params=pltpu.CompilerParams(
            collective_id=0, has_side_effects=True, vmem_limit_bytes=64 << 20
        ),
        cost_estimate=pl.CostEstimate(
            flops=12 * tokens * z.width * z.hidden + 16 * tokens * z.width * z.length // 16,
            bytes_accessed=40 * tokens * z.width,
            transcendentals=tokens * z.hidden,
        ),
    )(x, cot, shard_in, shard_out, shard_vec, *tables)


def nesterov(weight, moment, average, grad, rate, scale):
    scaled = grad * scale
    moment_new = MOMENTUM * moment + scaled
    weight_new = weight - rate * (scaled + MOMENTUM * moment_new)
    average_new = AVG_DECAY * average + (1.0 - AVG_DECAY) * weight_new
    return (moment_new, weight_new, average_new)


def on_device(
    seq_parts,
    batch_parts,
    layer_input_tokens,
    cotangent,
    weight_in,
    weight_out,
    bias_ff,
    norm_vec,
    moment_in,
    average_in,
    moment_out,
    average_out,
    moment_bias,
    average_bias,
    moment_norm,
    average_norm,
):
    seqs, local, width = layer_input_tokens.shape
    devices = seq_parts * batch_parts
    hidden = weight_out.shape[0] * devices
    z = Sizes(seq_parts, batch_parts, seqs, local, width, hidden)
    tokens = seqs * local

    shard_in = weight_in.T.astype(BF16)
    shard_out = weight_out if z.with_batch else weight_out.astype(BF16)
    bias_shard, norm_shard = bias_ff, norm_vec
    if not z.with_batch:
        shard_in, shard_out, bias_shard = (
            lax.all_gather(v, "batch", axis=0, tiled=True) for v in (shard_in, shard_out, bias_shard)
        )
        norm_shard = lax.all_gather(norm_shard, "batch", axis=1, tiled=True)
    bias_line = jnp.pad(bias_shard[None, :], ((0, 7), (0, LANES - bias_shard.shape[0])))
    norm_rows = jnp.pad(norm_shard, ((0, 3), (0, LANES - norm_shard.shape[1])))
    shard_vec = jnp.concatenate([bias_line, norm_rows], axis=0)

    tables = [jnp.asarray(sequence_tables(z))] + [jnp.asarray(t) for t in mixing_tables(z)]
    result, tokens_grad, grad_in, grad_out, grad_vec, _ = run_step(
        z,
        layer_input_tokens.reshape(tokens, width),
        cotangent.reshape(tokens, width),
        shard_in,
        shard_out,
        shard_vec,
        tables,
    )
    index = lax.axis_index("seq") * batch_parts + lax.axis_index("batch")
    if not z.with_batch:
        grad_in = lax.psum_scatter(grad_in, "batch", scatter_dimension=0, tiled=True)
        grad_out = lax.psum_scatter(grad_out, "batch", scatter_dimension=0, tiled=True)
        grad_vec = lax.psum(grad_vec, "batch")
    count, narrow = hidden // devices, width // devices
    grad_bias = lax.dynamic_slice(grad_vec[: z.chunks].reshape(hidden), (index * count,), (count,))
    grad_norm = lax.dynamic_slice(grad_vec[8:13], (0, index * narrow), (5, narrow))

    scale = (seqs * batch_parts * local * seq_parts) ** (-0.5)
    m_in, w_in_new, a_in = nesterov(
        weight_in, moment_in, average_in, grad_in.T, RATE_MATRIX, scale
    )
    m_out, w_out_new, a_out = nesterov(
        weight_out, moment_out, average_out, grad_out, RATE_MATRIX, scale
    )
    m_bias, b_new, a_bias = nesterov(
        bias_ff, moment_bias, average_bias, grad_bias, RATE_VECTOR, scale
    )
    m_norm, n_new, a_norm = nesterov(
        norm_vec, moment_norm, average_norm, grad_norm, RATE_VECTOR, scale
    )
    return (
        result.reshape(seqs, local, width),
        tokens_grad.reshape(seqs, local, width),
        m_in,
        w_in_new,
        a_in,
        m_out,
        w_out_new,
        a_out,
        m_bias,
        b_new,
        a_bias,
        m_norm,
        n_new,
        a_norm,
    )


def solution(mesh):
    tokens = P("batch", "seq", None)
    columns, rows, flat = P(None, ("seq", "batch")), P(("seq", "batch"), None), P(("seq", "batch"))
    return jax.shard_map(
        functools.partial(on_device, mesh.shape["seq"], mesh.shape["batch"]),
        mesh=mesh,
        in_specs=(tokens, tokens, columns, rows, flat, columns)
        + (columns, columns, rows, rows, flat, flat, columns, columns),
        out_specs=(tokens, tokens)
        + (columns,) * 3
        + (rows,) * 3
        + (flat,) * 3
        + (columns,) * 3,
        check_vma=False,
    )
```
